256 devices in a mesh: dp: 4 (over y), frame: 4 (over x), height: 16 (over z, core).
Axes of the slice: x: 4, y: 4, z: 8, core: 2. Of those that a mesh axis runs over, the one named last changes fastest.
Arguments:
- clip_latents: bfloat16 [4, 8, 32, 64, 384], P('dp', 'frame', 'height'), may hold values from -6 to 6
- conv_one: bfloat16 [3, 3, 3, 384, 384], replicated, may hold values from -0.0625 to 0.0625
- conv_two: bfloat16 [3, 3, 384, 192], replicated, may hold values from -0.109375 to 0.109375
- cotangent: bfloat16 [4, 8, 64, 128, 192], P('dp', 'frame', 'height'), may hold values from -6 to 6
Outputs:
- grad_latents: bfloat16 [4, 8, 32, 64, 384], P('dp', 'frame', 'height')
- grad_conv_one: float32 [3, 3, 3, 384, 384], P(None, None, None, ('dp', 'frame'), 'height')
- grad_conv_two: float32 [3, 3, 384, 192], P(None, None, ('dp', 'frame'), 'height')
The draws below stay inside these ranges and needn't reach their ends.
All inputs are finite; a program needn't handle non-finite values.
Results may differ from the reference program's by a relative error of at most 0.0049.
Values may be sent and summed in bfloat16 or wider, within the bound.
No kernel may reach another device: no remote copies, remote signals or barrier semaphores. Data moves between devices by JAX's collectives and lax.ppermute only.
A program may use at most 128 MiB of HBM per device.

```python
import jax
import jax.numpy as jnp
from jax import lax

C1 = 384
C2 = 192
WL = 64
CLIPS = 4
FRAMES = 8
ROWS = 32


def block_levels(stream_key, shape, cuts, low, high):
    def one(dim, parts):
        heights = jax.random.uniform(jax.random.fold_in(jax.random.fold_in(stream_key, 6), dim), (parts,), jnp.float32, low / len(cuts), high / len(cuts))
        return jnp.repeat(jnp.exp(heights), shape[dim] // parts).reshape((-1,) + (1,) * (len(shape) - dim - 1))

    level = one(*cuts[0])
    for cut in cuts[1:]:
        level = level * one(*cut)
    return level


def noise(own_key, shape, width, most, shards=(), kind=jnp.bfloat16):
    factor_of = block_levels(own_key, shape, shards, -0.22, 0.18) if shards else 1.0
    array = jax.random.normal(own_key, shape, jnp.float32) * width * factor_of
    return jnp.minimum(jnp.maximum(array, -most), most).astype(kind)


def setup_inputs(seed: int = 0) -> dict:
    key_of = jax.random.split(jax.random.key(seed), 5)
    return {
        "clip_latents": noise(key_of[0], (CLIPS, FRAMES, ROWS, WL, C1), 1.0, 6.0, ((0, 4), (1, 4), (2, 16))),
        "conv_one": noise(key_of[1], (3, 3, 3, C1, C1), (27 * C1) ** -0.5, 0.0625),
        "conv_two": noise(key_of[2], (3, 3, C1, C2), (9 * C1) ** -0.5, 0.109375),
        "cotangent": noise(key_of[3], (CLIPS, FRAMES, 2 * ROWS, 2 * WL, C2), 1.0, 6.0, ((0, 4), (1, 4), (2, 16))),
    }


def forward_taps(padded, weight, shape_out):
    frames_n, rows_n, cols_n = shape_out
    summed = jnp.zeros((frames_n, rows_n, cols_n, weight.shape[4]), jnp.float32)
    for frame_tap in range(3):
        for row_tap in range(3):
            for column_tap in range(3):
                window = padded[frame_tap:frame_tap + frames_n, row_tap:row_tap + rows_n, column_tap:column_tap + cols_n]
                summed = summed + jnp.einsum("frwc,cd->frwd", window.astype(jnp.float32), weight[frame_tap, row_tap, column_tap].astype(jnp.float32))
    return summed


def backward_taps(padded, weight, shape_out):
    frames_n, rows_n, cols_n = shape_out
    summed = jnp.zeros((frames_n, rows_n, cols_n, weight.shape[3]), jnp.float32)
    for frame_tap in range(3):
        for row_tap in range(3):
            for column_tap in range(3):
                window = padded[2 - frame_tap:2 - frame_tap + frames_n, 2 - row_tap:2 - row_tap + rows_n, 2 - column_tap:2 - column_tap + cols_n]
                summed = summed + jnp.einsum("frwd,cd->frwc", window.astype(jnp.float32), weight[frame_tap, row_tap, column_tap].astype(jnp.float32))
    return summed


def weight_taps(padded, grad_out):
    frames_n, rows_n, cols_n = grad_out.shape[:3]
    taps_list = []
    for frame_tap in range(3):
        for row_tap in range(3):
            for column_tap in range(3):
                window = padded[frame_tap:frame_tap + frames_n, row_tap:row_tap + rows_n, column_tap:column_tap + cols_n]
                taps_list.append(jnp.einsum("frwc,frwd->cd", window.astype(jnp.float32), grad_out.astype(jnp.float32)))
    stacked = jnp.stack(taps_list)
    return stacked.reshape((3, 3, 3) + stacked.shape[1:])


def plane_backward(padded, weight, shape_out):
    frames_n, rows_n, cols_n = shape_out
    summed = jnp.zeros((frames_n, rows_n, cols_n, weight.shape[2]), jnp.float32)
    for row_tap in range(3):
        for column_tap in range(3):
            window = padded[:, 2 - row_tap:2 - row_tap + rows_n, 2 - column_tap:2 - column_tap + cols_n]
            summed = summed + jnp.einsum("frwd,cd->frwc", window.astype(jnp.float32), weight[row_tap, column_tap].astype(jnp.float32))
    return summed


def plane_weight(padded, grad_out):
    frames_n, rows_n, cols_n = grad_out.shape[:3]
    taps_list = []
    for row_tap in range(3):
        for column_tap in range(3):
            window = padded[:, row_tap:row_tap + rows_n, column_tap:column_tap + cols_n]
            taps_list.append(jnp.einsum("frwc,frwd->cd", window.astype(jnp.float32), grad_out.astype(jnp.float32)))
    stacked = jnp.stack(taps_list)
    return stacked.reshape((3, 3) + stacked.shape[1:])


def per_clip(conv_one, conv_two, clip_in, upstream):
    frames_n, rows_n, cols_n = clip_in.shape[:3]
    padded_in = jnp.pad(clip_in, ((2, 0), (1, 1), (1, 1), (0, 0)))
    preact = forward_taps(padded_in, conv_one, (frames_n, rows_n, cols_n))
    hidden = jax.nn.silu(preact).astype(jnp.bfloat16)
    larger = jnp.repeat(jnp.repeat(hidden, 2, axis=1), 2, axis=2)
    padded_up = jnp.pad(larger, ((0, 0), (1, 1), (1, 1), (0, 0)))
    grad_two = plane_weight(padded_up, upstream)
    padded_cot = jnp.pad(upstream, ((0, 0), (1, 1), (1, 1), (0, 0)))
    grad_larger = plane_backward(padded_cot, conv_two, (frames_n, 2 * rows_n, 2 * cols_n))
    grad_hidden = grad_larger.reshape(frames_n, rows_n, 2, cols_n, 2, -1).sum(axis=(2, 4))
    sigma = jax.nn.sigmoid(preact)
    grad_pre = (grad_hidden * sigma * (1.0 + preact * (1.0 - sigma))).astype(jnp.bfloat16)
    grad_one = weight_taps(padded_in, grad_pre)
    padded_grad = jnp.pad(grad_pre, ((0, 2), (1, 1), (1, 1), (0, 0)))
    grad_in = backward_taps(padded_grad, conv_one, (frames_n, rows_n, cols_n)).astype(jnp.bfloat16)
    return grad_in, grad_one, grad_two


def reference(clip_latents, conv_one, conv_two, cotangent):
    def one_clip(pair):
        return per_clip(conv_one, conv_two, pair[0], pair[1])

    grad_in, grad_one, grad_two = lax.map(one_clip, (clip_latents, cotangent))
    return grad_in, jnp.sum(grad_one, axis=0), jnp.sum(grad_two, axis=0)
```

```python
import jax
import jax.numpy as jnp
from jax import lax
from jax.experimental import pallas as pl
from jax.experimental.pallas import tpu as pltpu
from jax.sharding import PartitionSpec as P

BF = jnp.bfloat16
F32 = jnp.float32
VMEM_LIMIT = 48 * 1024 * 1024


def params(**more):
    return pltpu.CompilerParams(vmem_limit_bytes=VMEM_LIMIT, **more)


def cost(macs, nbytes):
    return pl.CostEstimate(flops=2 * macs, bytes_accessed=nbytes, transcendentals=0)


def column_shifts(block):
    wide = block.astype(F32)
    row = lax.broadcasted_iota(jnp.int32, wide.shape, 0)
    before = jnp.where(row == 0, 0.0, pltpu.roll(wide, 1, 0))
    after = jnp.where(row == 63, 0.0, pltpu.roll(wide, 63, 0))
    return before.astype(BF), after.astype(BF)


def ext_row(own, other, up, down, frame, row):
    first, second = (other, own) if own is not None else (None, None)
    if row == 0:
        return up[frame]
    if row == 3:
        return down[frame]
    return first[frame, row - 1] if frame < 2 else second[frame - 2, row - 1]


def box_kernel(cot, up, down, w2, gcat, gh, taps):
    size = (64, 256)
    pos = lax.broadcasted_iota(jnp.int32, size, 1) & 127
    low = lax.broadcasted_iota(jnp.int32, size, 0)
    pick = []
    for k in range(3):
        offset = pos - 2 * low - 1 + k
        pick.append(jnp.where((offset == 0) | (offset == 1), 1.0, 0.0))
    pick = jnp.concatenate(pick, axis=0).astype(BF)

    def line(t, r):
        if r < 0:
            return up[t]
        if r > 3:
            return down[t]
        return cot[t, r]

    for t in range(2):
        for r in range(2):
            at = pl.ds((t * 2 + r) * 64, 64)
            for j in range(3):
                a = 2 * r + 1 - j
                pair = jnp.concatenate([line(t, a), line(t, a + 1)], axis=0)
                box = jnp.dot(pick, pair, preferred_element_type=F32).astype(BF)
                for k in range(3):
                    piece = box[k * 64 : (k + 1) * 64]
                    taps[j * 3 + k, at, :] = piece
                    gcat[at, pl.ds((j * 3 + k) * 192, 192)] = piece
    total = jnp.zeros((256, 384), F32)
    for n in range(9):
        total = total + lax.dot_general(
            taps[n], w2[n], (((1,), (1,)), ((), ())), preferred_element_type=F32
        )
    gh[...] = total


def box_sums(cot, up, down, w2):
    return pl.pallas_call(
        box_kernel,
        out_shape=(
            jax.ShapeDtypeStruct((256, 1728), BF),
            jax.ShapeDtypeStruct((256, 384), F32),
        ),
        scratch_shapes=[pltpu.VMEM((9, 256, 192), BF)],
        compiler_params=params(),
        cost_estimate=cost(300_000_000, 4_000_000),
        name="box_sums",
    )(cot, up, down, w2)


def forward_kernel(own, prev, up, down, w, gh, gp, gpt, ht, xx, acc):
    step = pl.program_id(0)

    @pl.when(step == 0)
    def _():
        for f in range(4):
            for r in range(4):
                block = ext_row(own, prev, up, down, f, r)
                before, after = column_shifts(block)
                xx[f, r, :, 0:384] = before
                xx[f, r, :, 384:768] = block
                xx[f, r, :, 768:1152] = after
        acc[...] = jnp.zeros_like(acc)

    i = step // 3
    j = step - 3 * i
    lhs = xx[pl.ds(i, 2), pl.ds(j, 2)].reshape(256, 1152)
    acc[...] += jnp.dot(lhs, w[0], preferred_element_type=F32)

    @pl.when(step == 8)
    def _():
        pre = acc[...]
        sigma = jax.nn.sigmoid(pre)
        hidden = pre * sigma
        grad = gh[...] * sigma * (1.0 + pre * (1.0 - sigma))
        gp[...] = grad.astype(BF).reshape(2, 2, 64, 384)
        grad_t = grad.T
        for b in range(16):
            gpt[b] = grad_t[b * 24 : (b + 1) * 24].astype(BF)
        ht[...] = hidden.T.astype(BF)


def whole(shape):
    return pl.BlockSpec(shape, lambda n: (0,) * len(shape))


def forward(own, prev, up, down, w, gh):
    return pl.pallas_call(
        forward_kernel,
        grid=(9,),
        in_specs=[
            whole((2, 2, 64, 384)),
            whole((2, 2, 64, 384)),
            whole((4, 64, 384)),
            whole((4, 64, 384)),
            pl.BlockSpec((1, 1152, 384), lambda n: (n, 0, 0)),
            whole((256, 384)),
        ],
        out_specs=(whole((2, 2, 64, 384)), whole((16, 24, 256)), whole((384, 256))),
        out_shape=(
            jax.ShapeDtypeStruct((2, 2, 64, 384), BF),
            jax.ShapeDtypeStruct((16, 24, 256), BF),
            jax.ShapeDtypeStruct((384, 256), BF),
        ),
        scratch_shapes=[pltpu.VMEM((4, 4, 64, 1152), BF), pltpu.VMEM((256, 384), F32)],
        compiler_params=params(),
        cost_estimate=cost(1_020_000_000, 10_000_000),
        name="forward",
    )(own, prev, up, down, w, gh)


def two_kernel(ht, gcat, out):
    res = jnp.dot(ht[...], gcat[...], preferred_element_type=F32)
    for b in range(16):
        out[b] = res[b * 24 : (b + 1) * 24].astype(BF)


def two_part(ht, gcat):
    return pl.pallas_call(
        two_kernel,
        out_shape=jax.ShapeDtypeStruct((16, 24, 1728), BF),
        compiler_params=params(),
        cost_estimate=cost(170_000_000, 3_000_000),
        name="two_part",
    )(ht, gcat)


def latents_kernel(own, after, up, down, w, out, gg, acc):
    step = pl.program_id(0)

    @pl.when(step == 0)
    def _():
        for f in range(4):
            for r in range(4):
                block = ext_row(after, own, up, down, f, r)
                before, later = column_shifts(block)
                gg[0, f, r] = later
                gg[1, f, r] = block
                gg[2, f, r] = before
        acc[...] = jnp.zeros_like(acc)

    i = step // 3
    j = step - 3 * i
    total = acc[...]
    for k in range(3):
        lhs = gg[k, pl.ds(2 - i, 2), pl.ds(2 - j, 2)].reshape(256, 384)
        total = total + lax.dot_general(
            lhs, w[0, k], (((1,), (1,)), ((), ())), preferred_element_type=F32
        )
    acc[...] = total

    @pl.when(step == 8)
    def _():
        out[...] = acc[...].astype(BF).reshape(2, 2, 64, 384)


def latents_grad(own, after, up, down, w):
    return pl.pallas_call(
        latents_kernel,
        grid=(9,),
        in_specs=[
            whole((2, 2, 64, 384)),
            whole((2, 2, 64, 384)),
            whole((4, 64, 384)),
            whole((4, 64, 384)),
            pl.BlockSpec((1, 3, 384, 384), lambda n: (n, 0, 0, 0)),
        ],
        out_specs=whole((2, 2, 64, 384)),
        out_shape=jax.ShapeDtypeStruct((2, 2, 64, 384), BF),
        scratch_shapes=[pltpu.VMEM((3, 4, 4, 64, 384), BF), pltpu.VMEM((256, 384), F32)],
        compiler_params=params(),
        cost_estimate=cost(1_020_000_000, 10_000_000),
        name="latents_grad",
    )(own, after, up, down, w)


def one_kernel(g, x, out, gs, acc):
    step = pl.program_id(0)

    @pl.when(step == 0)
    def _():
        acc[...] = jnp.zeros_like(acc)

    lane = lax.broadcasted_iota(jnp.int32, (24, 128), 1)
    col = lane & 63
    left = lane < 64

    def piece(h, f):
        mid = g[h, :, pl.ds(f * 128, 128)].astype(F32)
        later = jnp.where(col == 63, 0.0, pltpu.roll(mid, 127, 1))
        before = jnp.where(col == 0, 0.0, pltpu.roll(mid, 1, 1))
        return [later, mid, before]

    first = step * 4
    keep_top = (step > 0).astype(F32)
    keep_bottom = (step < 3).astype(F32)
    for f in range(4):
        cols = [[p * keep_top for p in piece(jnp.maximum(first - 1, 0), f)]]
        for h in range(4):
            cols.append(piece(first + h, f))
        cols.append([p * keep_bottom for p in piece(jnp.minimum(first + 4, 15), f)])
        for h in range(4):
            above, here, below = cols[h], cols[h + 1], cols[h + 2]
            rows = []
            for k in range(3):
                rows.append(pltpu.roll(jnp.where(left, below[k], here[k]), 64, 1))
            for k in range(3):
                rows.append(here[k])
            for k in range(3):
                rows.append(pltpu.roll(jnp.where(left, here[k], above[k]), 64, 1))
            rows.append(jnp.zeros((8, 128), F32))
            gs[f, :, pl.ds(h * 128, 128)] = jnp.concatenate(rows, axis=0).astype(BF)

    for s in range(2):
        xs = x[:, s].reshape(512, 384)
        lhs = gs[s : s + 3].reshape(672, 512)
        res = jnp.dot(lhs, xs, preferred_element_type=F32)
        for b in range(3):
            acc[b, 0:224] += res[b * 224 : (b + 1) * 224]

    @pl.when(step == 3)
    def _():
        for b in range(3):
            turned = acc[b].T
            for c in range(16):
                out[c, :, b * 256 : (b + 1) * 256] = turned[c * 24 : (c + 1) * 24].astype(BF)


def one_part(g, x):
    return pl.pallas_call(
        one_kernel,
        grid=(4,),
        in_specs=[
            whole((16, 24, 512)),
            pl.BlockSpec((4, 2, 2, 64, 384), lambda n: (n, 0, 0, 0, 0)),
        ],
        out_specs=whole((16, 24, 768)),
        out_shape=jax.ShapeDtypeStruct((16, 24, 768), BF),
        scratch_shapes=[pltpu.VMEM((4, 224, 512), BF), pltpu.VMEM((3, 256, 384), F32)],
        compiler_params=params(),
        cost_estimate=cost(1_020_000_000, 5_000_000),
        name="one_part",
    )(g, x)


def summed(ref):
    total = ref[0].astype(F32)
    for n in range(1, 16):
        total = total + ref[n].astype(F32)
    return total


def two_mid_kernel(parts, out):
    total = summed(parts)
    pad = jnp.zeros((24, 20), F32)
    for h in range(16):
        cut = [total[:, n * 192 + h * 12 : n * 192 + h * 12 + 12] for n in range(9)]
        out[h] = jnp.concatenate(cut + [pad], axis=1).astype(BF)


def two_mid(parts):
    return pl.pallas_call(
        two_mid_kernel,
        out_shape=jax.ShapeDtypeStruct((16, 24, 128), BF),
        compiler_params=params(),
        cost_estimate=cost(1_000_000, 1_500_000),
        name="two_mid",
    )(parts)


def final_one_kernel(parts, out):
    total = summed(parts)
    for i in range(3):
        for n in range(9):
            at = (2 - i) * 256 + n * 24
            out[i * 9 + n] = total[:, at : at + 24]


def final_one(parts):
    return pl.pallas_call(
        final_one_kernel,
        out_shape=jax.ShapeDtypeStruct((27, 24, 24), F32),
        compiler_params=params(),
        cost_estimate=cost(1_000_000, 800_000),
        name="final_one",
    )(parts)


def final_two_kernel(parts, out):
    total = summed(parts)
    for n in range(9):
        out[n] = total[:, n * 12 : (n + 1) * 12]


def final_two(parts):
    return pl.pallas_call(
        final_two_kernel,
        out_shape=jax.ShapeDtypeStruct((9, 24, 12), F32),
        compiler_params=params(),
        cost_estimate=cost(1_000_000, 200_000),
        name="final_two",
    )(parts)


def local(clip_latents, conv_one, conv_two, cotangent):
    x = clip_latents[0]
    cot = cotangent[0]
    heights = lax.axis_size("height")
    frames = lax.axis_size("frame")
    up_perm = [(n, n + 1) for n in range(heights - 1)]
    down_perm = [(n + 1, n) for n in range(heights - 1)]
    next_perm = [(n, n + 1) for n in range(frames - 1)]
    prev_perm = [(n + 1, n) for n in range(frames - 1)]

    x_all = lax.all_gather(x, "height", axis=0, tiled=False)

    x_prev = lax.ppermute(x, "frame", next_perm)
    cot_up = lax.ppermute(cot[:, 3], "height", up_perm)
    cot_down = lax.ppermute(cot[:, 0], "height", down_perm)
    x_up = lax.ppermute(jnp.concatenate([x_prev[:, 1], x[:, 1]], 0), "height", up_perm)
    x_down = lax.ppermute(jnp.concatenate([x_prev[:, 0], x[:, 0]], 0), "height", down_perm)

    gcat, gh = box_sums(cot, cot_up, cot_down, conv_two.reshape(9, 384, 192))
    gp, gpt, ht = forward(x, x_prev, x_up, x_down, conv_one.reshape(9, 1152, 384), gh)

    gpt_next = lax.ppermute(gpt, "frame", prev_perm)
    gp_next = gpt_next.reshape(384, 256).T.reshape(2, 2, 64, 384)
    g = lax.all_to_all(
        jnp.concatenate([gpt, gpt_next], axis=2), "height", 0, 0, tiled=True
    )
    g_up = lax.ppermute(jnp.concatenate([gp[:, 1], gp_next[:, 1]], 0), "height", up_perm)
    g_down = lax.ppermute(jnp.concatenate([gp[:, 0], gp_next[:, 0]], 0), "height", down_perm)

    two = two_part(ht, gcat)
    two = lax.all_to_all(two, ("dp", "frame"), 0, 0, tiled=True)
    grad_in = latents_grad(gp, gp_next, g_up, g_down, conv_one.reshape(9, 3, 384, 384))
    two = lax.all_to_all(two_mid(two), "height", 0, 0, tiled=True)

    one = lax.all_to_all(one_part(g, x_all), ("dp", "frame"), 0, 0, tiled=True)
    one = final_one(one).reshape(3, 3, 3, 24, 24)
    two = final_two(two).reshape(3, 3, 24, 12)
    return (grad_in[None], one, two)


def solution(mesh):
    placed = (
        P("dp", "frame", "height", None, None),
        P(),
        P(),
        P("dp", "frame", "height", None, None),
    )
    return jax.shard_map(
        local,
        mesh=mesh,
        in_specs=placed,
        out_specs=(
            P("dp", "frame", "height", None, None),
            P(None, None, None, ("dp", "frame"), "height"),
            P(None, None, ("dp", "frame"), "height"),
        ),
        check_vma=False,
    )
```

```python
import jax
import jax.numpy as jnp
from jax import lax
from jax.experimental import pallas as pl
from jax.experimental.pallas import tpu as pltpu
from jax.sharding import PartitionSpec as P

BF = jnp.bfloat16
F32 = jnp.float32
MIB = 1024 * 1024


def params(mib=16):
    return pltpu.CompilerParams(vmem_limit_bytes=mib * MIB)


def anywhere(count):
    return [pl.BlockSpec(memory_space=pl.ANY)] * count


def bring(sources, targets, sems):
    copies = [
        pltpu.make_async_copy(source, target, sems.at[n])
        for n, (source, target) in enumerate(zip(sources, targets))
    ]
    for each in copies:
        each.start()
    return copies


def vmem(count):
    return [pl.BlockSpec(memory_space=pltpu.VMEM)] * count


def cost(macs, nbytes):
    return pl.CostEstimate(flops=2 * macs, bytes_accessed=nbytes, transcendentals=0)


def column_shifts(wide):
    row = lax.broadcasted_iota(jnp.int32, wide.shape, 0)
    before = jnp.where(row == 0, 0.0, pltpu.roll(wide, 1, 0))
    after = jnp.where(row == 63, 0.0, pltpu.roll(wide, 63, 0))
    return before.astype(BF), after.astype(BF)


def place():
    height, frame = lax.axis_index("height"), lax.axis_index("frame")
    last = lax.axis_size("height") - 1, lax.axis_size("frame") - 1
    return (
        lax.rem(height, 2),
        (height > 0).astype(F32),
        (height < last[0]).astype(F32),
        (frame > 0).astype(F32),
        (frame < last[1]).astype(F32),
    )


def stack_columns(dest, low, high, cross, inner, at, oks, order):
    core, above_ok, below_ok = at[:3]
    for f in range(4):
        for r in range(4):
            keep = oks[f // 2]
            if r in (0, 3):
                pick_cross = core == (0 if r == 0 else 1)
                block = jnp.where(pick_cross, cross[f].astype(F32), inner[f].astype(F32))
                edge = above_ok if r == 0 else below_ok
                keep = edge if keep is None else edge * keep
            else:
                block = (low if f < 2 else high)[f % 2, r - 1].astype(F32)
            if keep is not None:
                block = block * keep
            before, after = column_shifts(block)
            sides = (before, after) if order > 0 else (after, before)
            dest[f, r, :, 0:384] = sides[0]
            dest[f, r, :, 384:768] = block.astype(BF)
            dest[f, r, :, 768:1152] = sides[1]


def load_kernel(w, out, sems):
    parts = [pl.ds(3 * n, 3) for n in range(9)]
    for each in bring([w.at[p] for p in parts], [out.at[p] for p in parts], sems):
        each.wait()


def load(w):
    return pl.pallas_call(
        load_kernel,
        in_specs=anywhere(1),
        out_specs=vmem(1)[0],
        out_shape=jax.ShapeDtypeStruct((27, 384, 384), BF),
        scratch_shapes=[pltpu.SemaphoreType.DMA((9,))],
        compiler_params=params(46),
        cost_estimate=cost(1000, 16_000_000),
        name="load",
    )(w)


def pair_kernel(own, other, cot, out, cross, inner):
    core = place()[0]
    out[core] = own[...]
    out[1 - core] = other[...]
    for target, line in ((cross, 3 * core), (inner, 3 - 3 * core)):
        for t in range(2):
            for n in range(3):
                target[t, :, n * 128 : (n + 1) * 128] = cot[t, line, n * 64 : (n + 1) * 64, :]


def pair(own, other, cot):
    rows = jax.ShapeDtypeStruct((2, 64, 384), BF)
    return pl.pallas_call(
        pair_kernel,
        in_specs=vmem(3),
        out_specs=tuple(vmem(3)),
        out_shape=(jax.ShapeDtypeStruct((2, 2, 2, 64, 384), BF), rows, rows),
        compiler_params=params(),
        cost_estimate=cost(1000, 1_600_000),
        name="pair",
    )(own, other, cot)


def edges_kernel(own, prev, cot_cross, cot_inner, cross, inner):
    core = place()[0]
    for out, row, lines in ((cross, core, cot_cross), (inner, 1 - core, cot_inner)):
        for t in range(2):
            out[t] = prev[t, row]
            out[2 + t] = own[t, row]
            out[4 + t] = lines[t]


def edges(own, prev, cot_cross, cot_inner):
    shape = jax.ShapeDtypeStruct((6, 64, 384), BF)
    return pl.pallas_call(
        edges_kernel,
        in_specs=vmem(4),
        out_specs=tuple(vmem(2)),
        out_shape=(shape, shape),
        compiler_params=params(),
        cost_estimate=cost(1000, 1_000_000),
        name="edges",
    )(own, prev, cot_cross, cot_inner)


def box_pick():
    size = (64, 256)
    pos = lax.broadcasted_iota(jnp.int32, size, 1) & 127
    low = lax.broadcasted_iota(jnp.int32, size, 0)
    pick = []
    for k in range(3):
        offset = pos - 2 * low - 1 + k
        pick.append(jnp.where((offset == 0) | (offset == 1), 1.0, 0.0))
    return jnp.concatenate(pick, axis=0).astype(BF)


def forward_kernel(own, prev, cross, inner, cotv, w2, wv, gp, gpt, ht, gcat, xx, w2v, sem):
    last = pltpu.make_async_copy(w2, w2v, sem)
    last.start()
    at = place()
    core, above_ok, below_ok, before_ok = at[:4]
    stack_columns(xx, prev, own, cross, inner, at, (before_ok, None), 1)

    def line(t, r):
        if 0 <= r < 4:
            return cotv[t, r]
        pick_cross = core == (0 if r < 0 else 1)
        row = jnp.where(pick_cross, cross[4 + t].astype(F32), inner[4 + t].astype(F32))
        row = (row * (above_ok if r < 0 else below_ok)).astype(BF)
        return jnp.concatenate([row[:, n * 128 : (n + 1) * 128] for n in range(3)], axis=0)

    pick = box_pick()
    for t in range(2):
        for r in range(2):
            rows = pl.ds((t * 2 + r) * 64, 64)
            for j in range(3):
                a = 2 * r + 1 - j
                pair = jnp.concatenate([line(t, a), line(t, a + 1)], axis=1)
                box = lax.dot_general(
                    pick, pair, (((1,), (1,)), ((), ())), preferred_element_type=F32
                ).astype(BF)
                for k in range(3):
                    gcat[rows, pl.ds((j * 3 + k) * 192, 192)] = box[k * 64 : (k + 1) * 64]
    pre = jnp.zeros((256, 384), F32)
    for n in range(9):
        i, j = n // 3, n % 3
        lhs = xx[i : i + 2, j : j + 2].reshape(256, 1152)
        rhs = wv[3 * n : 3 * n + 3].reshape(1152, 384)
        pre = pre + jnp.dot(lhs, rhs, preferred_element_type=F32)
    last.wait()
    gh = jnp.dot(gcat[...], w2v[...], preferred_element_type=F32)
    sigma = jax.nn.sigmoid(pre)
    hidden = pre * sigma
    grad = gh * sigma * (1.0 + pre * (1.0 - sigma))
    gp[...] = grad.astype(BF).reshape(2, 2, 64, 384)
    grad_t = grad.T
    for b in range(16):
        gpt[b] = grad_t[b * 24 : (b + 1) * 24].astype(BF)
    ht[...] = hidden.T.astype(BF)


def forward(own, prev, cross, inner, cot, w2, w):
    return pl.pallas_call(
        forward_kernel,
        in_specs=vmem(5) + anywhere(1) + vmem(1),
        out_specs=tuple(vmem(4)),
        out_shape=(
            jax.ShapeDtypeStruct((2, 2, 64, 384), BF),
            jax.ShapeDtypeStruct((16, 24, 256), BF),
            jax.ShapeDtypeStruct((384, 256), BF),
            jax.ShapeDtypeStruct((256, 1728), BF),
        ),
        scratch_shapes=[
            pltpu.VMEM((4, 4, 64, 1152), BF),
            pltpu.VMEM((1728, 384), BF),
            pltpu.SemaphoreType.DMA,
        ],
        compiler_params=params(24),
        cost_estimate=cost(1_300_000_000, 12_000_000),
        name="forward",
    )(own, prev, cross, inner, cot, w2, w)


def mix_kernel(own, after, own_t, by_channel, cross, inner):
    at = place()
    core, after_ok = at[0], at[4]
    later = (after[...].reshape(256, 384).astype(F32) * after_ok).T
    for b in range(16):
        by_channel[b, :, 0:256] = own_t[b]
        by_channel[b, :, 256:512] = later[b * 24 : (b + 1) * 24].astype(BF)
    for out, row in ((cross, core), (inner, 1 - core)):
        for t in range(2):
            out[t] = own[t, row]
            out[2 + t] = after[t, row]


def mix(own, after, own_t):
    shape = jax.ShapeDtypeStruct((4, 64, 384), BF)
    return pl.pallas_call(
        mix_kernel,
        in_specs=vmem(3),
        out_specs=tuple(vmem(3)),
        out_shape=(jax.ShapeDtypeStruct((16, 24, 512), BF), shape, shape),
        compiler_params=params(),
        cost_estimate=cost(1000, 1_500_000),
        name="mix",
    )(own, after, own_t)


def two_kernel(ht, gcat, out):
    res = jnp.dot(ht[...], gcat[...], preferred_element_type=F32)
    for b in range(16):
        out[b] = res[b * 24 : (b + 1) * 24].astype(BF)


def two_part(ht, gcat):
    return pl.pallas_call(
        two_kernel,
        out_shape=jax.ShapeDtypeStruct((16, 24, 1728), BF),
        compiler_params=params(),
        cost_estimate=cost(170_000_000, 3_000_000),
        name="two_part",
    )(ht, gcat)


def latents_kernel(own, after, cross, inner, wv, out, gg):
    at = place()
    stack_columns(gg, own, after, cross, inner, at, (None, at[4]), -1)
    total = jnp.zeros((256, 384), F32)
    for n in range(9):
        i, j = n // 3, n % 3
        lhs = gg[2 - i : 4 - i, 2 - j : 4 - j].reshape(256, 1152)
        rhs = jnp.concatenate([wv[3 * n], wv[3 * n + 1], wv[3 * n + 2]], axis=1)
        total = total + lax.dot_general(
            lhs, rhs, (((1,), (1,)), ((), ())), preferred_element_type=F32
        )
    out[...] = total.astype(BF).reshape(2, 2, 64, 384)


def latents_grad(own, after, cross, inner, w):
    return pl.pallas_call(
        latents_kernel,
        in_specs=vmem(5),
        out_specs=vmem(1)[0],
        out_shape=jax.ShapeDtypeStruct((2, 2, 64, 384), BF),
        scratch_shapes=[
            pltpu.VMEM((4, 4, 64, 1152), BF),
        ],
        compiler_params=params(24),
        cost_estimate=cost(1_020_000_000, 10_000_000),
        name="latents_grad",
    )(own, after, cross, inner, w)


def one_kernel(g, *rest):
    blocks, (out, gs, cols, xv, sems) = rest[:8], rest[8:]
    arrive = bring(blocks, [xv.at[n] for n in range(8)], sems)
    lane = lax.broadcasted_iota(jnp.int32, (24, 128), 1)
    col = lane & 63
    left = lane < 64
    height = lax.axis_index("height")
    chip = height // 2
    way = 1 - 2 * (height - 2 * chip)

    cols[0] = jnp.zeros((4, 3, 24, 128), F32)
    cols[17] = jnp.zeros((4, 3, 24, 128), F32)
    for h in range(16):
        for f in range(4):
            mid = g[h, :, pl.ds(f * 128, 128)].astype(F32)
            cols[h + 1, f, 0] = jnp.where(col == 63, 0.0, pltpu.roll(mid, 127, 1))
            cols[h + 1, f, 1] = mid
            cols[h + 1, f, 2] = jnp.where(col == 0, 0.0, pltpu.roll(mid, 1, 1))
    for n, steps in enumerate((0, -1, -2, -3, 4, 1, 2, 3)):
        at = 2 * lax.rem(chip + way * steps + 16, 8)
        for f in range(4):
            lines = [[cols[at + m, f, k] for k in range(3)] for m in range(4)]
            for m in range(2):
                above, here, below = lines[m : m + 3]
                rows = [pltpu.roll(jnp.where(left, b, a), 64, 1) for a, b in zip(here, below)]
                rows += here
                rows += [pltpu.roll(jnp.where(left, b, a), 64, 1) for a, b in zip(above, here)]
                rows.append(jnp.zeros((8, 128), F32))
                to = pl.ds((2 * n + m) * 128, 128)
                gs[f, :, to] = jnp.concatenate(rows, axis=0).astype(BF)

    for each in arrive:
        each.wait()
    total = jnp.zeros((672, 384), F32)
    for s in range(2):
        xs = xv[:, :, s].reshape(2048, 384)
        lhs = gs[s : s + 3].reshape(672, 2048)
        total = total + jnp.dot(lhs, xs, preferred_element_type=F32)
    pad = jnp.zeros((32, 384), F32)
    for b in range(3):
        turned = jnp.concatenate([total[b * 224 : (b + 1) * 224], pad], axis=0).T
        for c in range(16):
            out[c, :, b * 256 : (b + 1) * 256] = turned[c * 24 : (c + 1) * 24].astype(BF)


def one_part(g, blocks):
    return pl.pallas_call(
        one_kernel,
        in_specs=vmem(1) + anywhere(8),
        out_specs=vmem(1)[0],
        out_shape=jax.ShapeDtypeStruct((16, 24, 768), BF),
        scratch_shapes=[
            pltpu.VMEM((4, 224, 2048), BF),
            pltpu.VMEM((18, 4, 3, 24, 128), F32),
            pltpu.VMEM((8, 2, 2, 2, 64, 384), BF),
            pltpu.SemaphoreType.DMA((8,)),
        ],
        compiler_params=params(24),
        cost_estimate=cost(1_020_000_000, 5_000_000),
        name="one_part",
    )(g, *blocks)


def summed(ref):
    total = ref[0].astype(F32)
    for n in range(1, 16):
        total = total + ref[n].astype(F32)
    return total


def two_mid_kernel(parts, out):
    total = summed(parts)
    pad = jnp.zeros((24, 20), F32)
    for h in range(16):
        cut = [total[:, n * 192 + h * 12 : n * 192 + h * 12 + 12] for n in range(9)]
        out[h] = jnp.concatenate(cut + [pad], axis=1).astype(BF)


def two_mid(parts):
    return pl.pallas_call(
        two_mid_kernel,
        out_shape=jax.ShapeDtypeStruct((16, 24, 128), BF),
        compiler_params=params(),
        cost_estimate=cost(1_000_000, 1_500_000),
        name="two_mid",
    )(parts)


def final_one_kernel(parts, out):
    total = summed(parts)
    for i in range(3):
        for n in range(9):
            at = (2 - i) * 256 + n * 24
            out[i * 9 + n] = total[:, at : at + 24]


def final_one(parts):
    return pl.pallas_call(
        final_one_kernel,
        out_shape=jax.ShapeDtypeStruct((27, 24, 24), F32),
        compiler_params=params(),
        cost_estimate=cost(1_000_000, 800_000),
        name="final_one",
    )(parts)


def final_two_kernel(parts, out):
    turned = summed(parts).T
    for n in range(9):
        out[n] = turned[n * 12 : (n + 1) * 12]


def final_two(parts):
    return pl.pallas_call(
        final_two_kernel,
        out_shape=jax.ShapeDtypeStruct((9, 12, 24), F32),
        compiler_params=params(),
        cost_estimate=cost(1_000_000, 200_000),
        name="final_two",
    )(parts)


def local(clip_latents, conv_one, conv_two, cotangent):
    x = clip_latents[0]
    cot = cotangent[0]
    heights = lax.axis_size("height")
    frames = lax.axis_size("frame")
    next_perm = [(n, (n + 1) % frames) for n in range(frames)]
    prev_perm = [((n + 1) % frames, n) for n in range(frames)]
    inner_perm = [(n, n ^ 1) for n in range(heights)]
    cross_perm = [(n, (n + 1 if n % 2 else n - 1) % heights) for n in range(heights)]
    ring_perm = [(n, (n - 2 if n % 2 else n + 2) % heights) for n in range(heights)]

    def inside(value):
        return lax.ppermute(value, "height", inner_perm)

    def across(value):
        return lax.ppermute(value, "height", cross_perm)

    def ring(value):
        return lax.ppermute(value, "height", ring_perm)

    cot = jnp.swapaxes(cot, 2, 3)
    w1 = conv_one.reshape(27, 384, 384)
    w2 = jnp.swapaxes(conv_two, 2, 3).reshape(1728, 384)
    x_prev = lax.ppermute(x, "frame", next_perm)
    pair0, cot_cross, cot_inner = pair(x, inside(x), cot)
    pair1 = ring(pair0)
    cross, inner = edges(x, x_prev, cot_cross, cot_inner)
    w1, cross, inner = lax.optimization_barrier((w1, cross, inner))
    w1 = load(w1)
    cross, inner = across(cross), inside(inner)
    pair1, w1, cross, inner = lax.optimization_barrier((pair1, w1, cross, inner))
    pair2 = ring(pair1)
    gp, gpt, ht, gcat = forward(x, x_prev, cross, inner, cot, w2, w1)

    gp_next = lax.ppermute(gp, "frame", prev_perm)
    gpt, pair1, pair2 = lax.optimization_barrier((gpt, pair1, pair2))
    pair3 = ring(pair2)
    by_channel, cross, inner = mix(gp, gp_next, gpt)
    by_channel, cross, inner, ht, pair3 = lax.optimization_barrier(
        (by_channel, cross, inner, ht, pair3)
    )
    g = lax.all_to_all(by_channel, "height", 0, 0, tiled=True)
    cross, inner = across(cross), inside(inner)
    pair4 = ring(pair3)
    two = two_part(ht, gcat)
    two = lax.all_to_all(two, ("dp", "frame"), 0, 0, tiled=True)
    g, pair4 = lax.optimization_barrier((g, pair4))
    blocks = (pair0, pair1, pair2, pair3, pair4, inside(pair1), inside(pair2), inside(pair3))

    one = one_part(g, blocks)
    one, cross, inner = lax.optimization_barrier((one, cross, inner))
    one = lax.all_to_all(one, ("dp", "frame"), 0, 0, tiled=True)
    grad_in = latents_grad(gp, gp_next, cross, inner, w1)
    grad_in, two = lax.optimization_barrier((grad_in, two))
    two = lax.all_to_all(two_mid(two), "height", 0, 0, tiled=True)
    one = final_one(one).reshape(3, 3, 3, 24, 24)
    two = jnp.swapaxes(final_two(two).reshape(3, 3, 12, 24), 2, 3)
    return (grad_in[None], one, two)


def solution(mesh):
    placed = (
        P("dp", "frame", "height", None, None),
        P(),
        P(),
        P("dp", "frame", "height", None, None),
    )
    return jax.shard_map(
        local,
        mesh=mesh,
        in_specs=placed,
        out_specs=(
            P("dp", "frame", "height", None, None),
            P(None, None, None, ("dp", "frame"), "height"),
            P(None, None, ("dp", "frame"), "height"),
        ),
        check_vma=False,
    )
```

```python
import jax
import jax.numpy as jnp
from jax import lax
from jax.experimental import pallas as pl
from jax.experimental.pallas import tpu as pltpu
from jax.sharding import PartitionSpec as P

BF = jnp.bfloat16
F32 = jnp.float32
MIB = 1024 * 1024


def params(mib=16):
    return pltpu.CompilerParams(vmem_limit_bytes=mib * MIB)


def anywhere(count):
    return [pl.BlockSpec(memory_space=pl.ANY)] * count


def bring(sources, targets, sems):
    copies = [
        pltpu.make_async_copy(source, target, sems.at[n])
        for n, (source, target) in enumerate(zip(sources, targets))
    ]
    for each in copies:
        each.start()
    return copies


def vmem(count):
    return [pl.BlockSpec(memory_space=pltpu.VMEM)] * count


def cost(macs, nbytes):
    return pl.CostEstimate(flops=2 * macs, bytes_accessed=nbytes, transcendentals=0)


def column_shifts(wide):
    row = lax.broadcasted_iota(jnp.int32, wide.shape, 0)
    before = jnp.where(row == 0, 0.0, pltpu.roll(wide, 1, 0))
    after = jnp.where(row == 63, 0.0, pltpu.roll(wide, 63, 0))
    return before.astype(BF), after.astype(BF)


def place():
    height, frame = lax.axis_index("height"), lax.axis_index("frame")
    last = lax.axis_size("height") - 1, lax.axis_size("frame") - 1
    return (
        lax.rem(height, 2),
        (height > 0).astype(F32),
        (height < last[0]).astype(F32),
        (frame > 0).astype(F32),
        (frame < last[1]).astype(F32),
    )


def stack_columns(dest, low, high, cross, inner, at, oks, order):
    core, above_ok, below_ok = at[:3]
    for f in range(4):
        for r in range(4):
            keep = oks[f // 2]
            if r in (0, 3):
                pick_cross = core == (0 if r == 0 else 1)
                block = jnp.where(pick_cross, cross[f].astype(F32), inner[f].astype(F32))
                edge = above_ok if r == 0 else below_ok
                keep = edge if keep is None else edge * keep
            else:
                block = (low if f < 2 else high)[f % 2, r - 1].astype(F32)
            if keep is not None:
                block = block * keep
            before, after = column_shifts(block)
            sides = (before, after) if order > 0 else (after, before)
            dest[f, r, :, 0:384] = sides[0]
            dest[f, r, :, 384:768] = block.astype(BF)
            dest[f, r, :, 768:1152] = sides[1]


def load_kernel(w, out, sems):
    parts = [pl.ds(3 * n, 3) for n in range(9)]
    for each in bring([w.at[p] for p in parts], [out.at[p] for p in parts], sems):
        each.wait()


def load(w):
    return pl.pallas_call(
        load_kernel,
        in_specs=anywhere(1),
        out_specs=vmem(1)[0],
        out_shape=jax.ShapeDtypeStruct((27, 384, 384), BF),
        scratch_shapes=[pltpu.SemaphoreType.DMA((9,))],
        compiler_params=params(46),
        cost_estimate=cost(1000, 16_000_000),
        name="load",
    )(w)


def pair_kernel(own, other, cot, out, cross, inner):
    core = place()[0]
    out[core] = own[...]
    out[1 - core] = other[...]
    for target, line in ((cross, 3 * core), (inner, 3 - 3 * core)):
        for t in range(2):
            for n in range(3):
                target[t, :, n * 128 : (n + 1) * 128] = cot[t, line, n * 64 : (n + 1) * 64, :]


def pair(own, other, cot):
    rows = jax.ShapeDtypeStruct((2, 64, 384), BF)
    return pl.pallas_call(
        pair_kernel,
        in_specs=vmem(3),
        out_specs=tuple(vmem(3)),
        out_shape=(jax.ShapeDtypeStruct((2, 2, 2, 64, 384), BF), rows, rows),
        compiler_params=params(),
        cost_estimate=cost(1000, 1_600_000),
        name="pair",
    )(own, other, cot)


def edges_kernel(own, prev, cot_cross, cot_inner, cross, inner):
    core = place()[0]
    for out, row, lines in ((cross, core, cot_cross), (inner, 1 - core, cot_inner)):
        for t in range(2):
            out[t] = prev[t, row]
            out[2 + t] = own[t, row]
            out[4 + t] = lines[t]


def edges(own, prev, cot_cross, cot_inner):
    shape = jax.ShapeDtypeStruct((6, 64, 384), BF)
    return pl.pallas_call(
        edges_kernel,
        in_specs=vmem(4),
        out_specs=tuple(vmem(2)),
        out_shape=(shape, shape),
        compiler_params=params(),
        cost_estimate=cost(1000, 1_000_000),
        name="edges",
    )(own, prev, cot_cross, cot_inner)


def box_pick():
    size = (64, 256)
    pos = lax.broadcasted_iota(jnp.int32, size, 1) & 127
    low = lax.broadcasted_iota(jnp.int32, size, 0)
    pick = []
    for k in range(3):
        offset = pos - 2 * low - 1 + k
        pick.append(jnp.where((offset == 0) | (offset == 1), 1.0, 0.0))
    return jnp.concatenate(pick, axis=0).astype(BF)


def forward_kernel(
    own, prev, cross, inner, cotv, w2, wv, gp, gpt, ht, keep, give, xx, gcat, w2v, sems
):
    last = bring([w2.at[:, pl.ds(0, 96)], w2.at[:, pl.ds(96, 96)]], [w2v.at[0], w2v.at[1]], sems)
    at = place()
    core, above_ok, below_ok, before_ok = at[:4]
    stack_columns(xx, prev, own, cross, inner, at, (before_ok, None), 1)

    def line(t, r):
        if 0 <= r < 4:
            return cotv[t, r]
        pick_cross = core == (0 if r < 0 else 1)
        row = jnp.where(pick_cross, cross[4 + t].astype(F32), inner[4 + t].astype(F32))
        row = (row * (above_ok if r < 0 else below_ok)).astype(BF)
        return jnp.concatenate([row[:, n * 128 : (n + 1) * 128] for n in range(3)], axis=0)

    pick = box_pick()
    for t in range(2):
        for r in range(2):
            rows = pl.ds((t * 2 + r) * 64, 64)
            for j in range(3):
                a = 2 * r + 1 - j
                pair = jnp.concatenate([line(t, a), line(t, a + 1)], axis=1)
                box = lax.dot_general(
                    pick, pair, (((1,), (1,)), ((), ())), preferred_element_type=F32
                ).astype(BF)
                for k in range(3):
                    for half in range(2):
                        piece = box[k * 64 : (k + 1) * 64, half * 96 : half * 96 + 96]
                        gcat[half, rows, pl.ds((j * 3 + k) * 96, 96)] = piece
    pre = jnp.zeros((256, 384), F32)
    for n in range(9):
        i, j = n // 3, n % 3
        lhs = xx[i : i + 2, j : j + 2].reshape(256, 1152)
        rhs = wv[3 * n : 3 * n + 3].reshape(1152, 384)
        pre = pre + jnp.dot(lhs, rhs, preferred_element_type=F32)
    keep[...] = gcat[core]
    give[...] = gcat[1 - core]
    for each in last:
        each.wait()
    gh = jnp.zeros((256, 384), F32)
    for half in range(2):
        rhs = w2v[half].reshape(864, 384)
        gh = gh + jnp.dot(gcat[half], rhs, preferred_element_type=F32)
    sigma = jax.nn.sigmoid(pre)
    hidden = pre * sigma
    grad = gh * sigma * (1.0 + pre * (1.0 - sigma))
    gp[...] = grad.astype(BF).reshape(2, 2, 64, 384)
    grad_t = grad.T
    for b in range(16):
        gpt[b] = grad_t[b * 24 : (b + 1) * 24].astype(BF)
    ht[...] = hidden.T.astype(BF)


def forward(own, prev, cross, inner, cot, w2, w):
    return pl.pallas_call(
        forward_kernel,
        in_specs=vmem(5) + anywhere(1) + vmem(1),
        out_specs=tuple(vmem(5)),
        out_shape=(
            jax.ShapeDtypeStruct((2, 2, 64, 384), BF),
            jax.ShapeDtypeStruct((16, 24, 256), BF),
            jax.ShapeDtypeStruct((384, 256), BF),
            jax.ShapeDtypeStruct((256, 864), BF),
            jax.ShapeDtypeStruct((256, 864), BF),
        ),
        scratch_shapes=[
            pltpu.VMEM((4, 4, 64, 1152), BF),
            pltpu.VMEM((2, 256, 864), BF),
            pltpu.VMEM((2, 9, 96, 384), BF),
            pltpu.SemaphoreType.DMA((2,)),
        ],
        compiler_params=params(14),
        cost_estimate=cost(1_300_000_000, 12_000_000),
        name="forward",
    )(own, prev, cross, inner, cot, w2, w)


def rows_kernel(own, after, cross, inner):
    core = place()[0]
    for out, row in ((cross, core), (inner, 1 - core)):
        for t in range(2):
            out[t] = own[t, row]
            out[2 + t] = after[t, row]


def rows(own, after):
    shape = jax.ShapeDtypeStruct((4, 64, 384), BF)
    return pl.pallas_call(
        rows_kernel,
        in_specs=vmem(2),
        out_specs=tuple(vmem(2)),
        out_shape=(shape, shape),
        compiler_params=params(),
        cost_estimate=cost(1000, 800_000),
        name="rows",
    )(own, after)


def two_kernel(ht, keep, ht_other, given, out):
    res = jnp.dot(ht[...], keep[...], preferred_element_type=F32)
    res = res + jnp.dot(ht_other[...], given[...], preferred_element_type=F32)
    for b in range(16):
        out[b] = res[b * 24 : (b + 1) * 24].astype(BF)


def two_part(ht, keep, ht_other, given):
    return pl.pallas_call(
        two_kernel,
        in_specs=vmem(4),
        out_specs=vmem(1)[0],
        out_shape=jax.ShapeDtypeStruct((16, 24, 864), BF),
        compiler_params=params(),
        cost_estimate=cost(170_000_000, 3_000_000),
        name="two_part",
    )(ht, keep, ht_other, given)


def latents_kernel(own, after, cross, inner, wv, out, gg):
    at = place()
    stack_columns(gg, own, after, cross, inner, at, (None, at[4]), -1)
    total = jnp.zeros((256, 384), F32)
    for n in range(9):
        i, j = n // 3, n % 3
        lhs = gg[2 - i : 4 - i, 2 - j : 4 - j].reshape(256, 1152)
        rhs = jnp.concatenate([wv[3 * n], wv[3 * n + 1], wv[3 * n + 2]], axis=1)
        total = total + lax.dot_general(
            lhs, rhs, (((1,), (1,)), ((), ())), preferred_element_type=F32
        )
    out[...] = total.astype(BF).reshape(2, 2, 64, 384)


def latents_grad(own, after, cross, inner, w):
    return pl.pallas_call(
        latents_kernel,
        in_specs=vmem(5),
        out_specs=vmem(1)[0],
        out_shape=jax.ShapeDtypeStruct((2, 2, 64, 384), BF),
        scratch_shapes=[
            pltpu.VMEM((4, 4, 64, 1152), BF),
        ],
        compiler_params=params(12),
        cost_estimate=cost(1_020_000_000, 10_000_000),
        name="latents_grad",
    )(own, after, cross, inner, w)


def one_kernel(g_in, g_after_in, *rest):
    blocks, (out, gs, cols, xv, g, g_after, sems) = rest[:8], rest[8:]
    arrive = bring(
        (g_in, g_after_in) + blocks, [g, g_after] + [xv.at[n] for n in range(8)], sems
    )
    arrive[0].wait()
    arrive[1].wait()
    lane = lax.broadcasted_iota(jnp.int32, (24, 128), 1)
    col = lane & 63
    left = lane < 64
    height = lax.axis_index("height")
    chip = height // 2
    way = 1 - 2 * (height - 2 * chip)

    after_ok = place()[4]
    cols[0] = jnp.zeros((4, 3, 24, 128), F32)
    cols[17] = jnp.zeros((4, 3, 24, 128), F32)
    for h in range(16):
        for f in range(4):
            mid = (g if f < 2 else g_after)[h, :, pl.ds(f % 2 * 128, 128)].astype(F32)
            mid = mid if f < 2 else mid * after_ok
            cols[h + 1, f, 0] = jnp.where(col == 63, 0.0, pltpu.roll(mid, 127, 1))
            cols[h + 1, f, 1] = mid
            cols[h + 1, f, 2] = jnp.where(col == 0, 0.0, pltpu.roll(mid, 1, 1))
    for n, steps in enumerate((0, -1, -2, -3, 4, 1, 2, 3)):
        at = 2 * lax.rem(chip + way * steps + 16, 8)
        for f in range(4):
            lines = [[cols[at + m, f, k] for k in range(3)] for m in range(4)]
            for m in range(2):
                above, here, below = lines[m : m + 3]
                rows = [pltpu.roll(jnp.where(left, b, a), 64, 1) for a, b in zip(here, below)]
                rows += here
                rows += [pltpu.roll(jnp.where(left, b, a), 64, 1) for a, b in zip(above, here)]
                rows.append(jnp.zeros((8, 128), F32))
                to = pl.ds((2 * n + m) * 128, 128)
                gs[f, :, to] = jnp.concatenate(rows, axis=0).astype(BF)

    for each in arrive[2:]:
        each.wait()
    total = jnp.zeros((672, 384), F32)
    for s in range(2):
        xs = xv[:, :, s].reshape(2048, 384)
        lhs = gs[s : s + 3].reshape(672, 2048)
        total = total + jnp.dot(lhs, xs, preferred_element_type=F32)
    pad = jnp.zeros((32, 384), F32)
    for b in range(3):
        turned = jnp.concatenate([total[b * 224 : (b + 1) * 224], pad], axis=0).T
        for c in range(16):
            out[c, :, b * 256 : (b + 1) * 256] = turned[c * 24 : (c + 1) * 24].astype(BF)


def one_part(g, g_after, blocks):
    return pl.pallas_call(
        one_kernel,
        in_specs=anywhere(10),
        out_specs=vmem(1)[0],
        out_shape=jax.ShapeDtypeStruct((16, 24, 768), BF),
        scratch_shapes=[
            pltpu.VMEM((4, 224, 2048), BF),
            pltpu.VMEM((18, 4, 3, 24, 128), F32),
            pltpu.VMEM((8, 2, 2, 2, 64, 384), BF),
            pltpu.VMEM((16, 24, 256), BF),
            pltpu.VMEM((16, 24, 256), BF),
            pltpu.SemaphoreType.DMA((10,)),
        ],
        compiler_params=params(20),
        cost_estimate=cost(1_020_000_000, 5_000_000),
        name="one_part",
    )(g, g_after, *blocks)


def summed(ref):
    total = ref[0].astype(F32)
    for n in range(1, 16):
        total = total + ref[n].astype(F32)
    return total


def two_mid_kernel(parts, out):
    core = place()[0]
    total = summed(parts)
    pad = jnp.zeros((24, 20), F32)
    for h in range(8):
        cut = [total[:, n * 96 + h * 12 : n * 96 + h * 12 + 12] for n in range(9)]
        out[core * 8 + h] = jnp.concatenate(cut + [pad], axis=1).astype(BF)
        out[8 - core * 8 + h] = jnp.zeros((24, 128), BF)


def two_mid(parts):
    return pl.pallas_call(
        two_mid_kernel,
        out_shape=jax.ShapeDtypeStruct((16, 24, 128), BF),
        compiler_params=params(),
        cost_estimate=cost(1_000_000, 1_500_000),
        name="two_mid",
    )(parts)


def final_one_kernel(parts, out):
    total = summed(parts)
    for i in range(3):
        for n in range(9):
            at = (2 - i) * 256 + n * 24
            out[i * 9 + n] = total[:, at : at + 24]


def final_one(parts):
    return pl.pallas_call(
        final_one_kernel,
        out_shape=jax.ShapeDtypeStruct((27, 24, 24), F32),
        compiler_params=params(),
        cost_estimate=cost(1_000_000, 800_000),
        name="final_one",
    )(parts)


def final_two_kernel(parts, out):
    turned = summed(parts).T
    for n in range(9):
        out[n] = turned[n * 12 : (n + 1) * 12]


def final_two(parts):
    return pl.pallas_call(
        final_two_kernel,
        out_shape=jax.ShapeDtypeStruct((9, 12, 24), F32),
        compiler_params=params(),
        cost_estimate=cost(1_000_000, 200_000),
        name="final_two",
    )(parts)


def local(clip_latents, conv_one, conv_two, cotangent):
    x = clip_latents[0]
    cot = cotangent[0]
    heights = lax.axis_size("height")
    frames = lax.axis_size("frame")
    next_perm = [(n, (n + 1) % frames) for n in range(frames)]
    prev_perm = [((n + 1) % frames, n) for n in range(frames)]
    inner_perm = [(n, n ^ 1) for n in range(heights)]
    cross_perm = [(n, (n + 1 if n % 2 else n - 1) % heights) for n in range(heights)]
    ring_perm = [(n, (n - 2 if n % 2 else n + 2) % heights) for n in range(heights)]

    def inside(value):
        return lax.ppermute(value, "height", inner_perm)

    def across(value):
        return lax.ppermute(value, "height", cross_perm)

    def ring(value):
        return lax.ppermute(value, "height", ring_perm)

    cot = jnp.swapaxes(cot, 2, 3)
    w1 = conv_one.reshape(27, 384, 384)
    w2 = jnp.swapaxes(conv_two, 2, 3).reshape(9, 192, 384)
    x_prev = lax.ppermute(x, "frame", next_perm)
    pair0, cot_cross, cot_inner = pair(x, inside(x), cot)
    pair1 = ring(pair0)
    cross, inner = edges(x, x_prev, cot_cross, cot_inner)
    w1_first, cross, inner = lax.optimization_barrier((w1, cross, inner))
    w1_first = load(w1_first)
    cross, inner = across(cross), inside(inner)
    pair1, w1_first, cross, inner = lax.optimization_barrier((pair1, w1_first, cross, inner))
    pair2 = ring(pair1)
    gp, gpt, ht, keep, give = forward(x, x_prev, cross, inner, cot, w2, w1_first)

    gp_next = lax.ppermute(gp, "frame", prev_perm)
    g = lax.all_to_all(gpt, "height", 0, 0, tiled=True)
    pair2, _ = lax.optimization_barrier((pair2, gp_next))
    pair3 = ring(pair2)
    ht_other, given = inside(ht), inside(give)
    cross, inner = rows(gp, gp_next)
    cross, inner = across(cross), inside(inner)
    g_next = lax.ppermute(g, "frame", prev_perm)
    ht, _, _ = lax.optimization_barrier((ht, gp_next, g))
    two = two_part(ht, keep, ht_other, given)
    w1, two = lax.optimization_barrier((w1, two))
    two = lax.all_to_all(two, ("dp", "frame"), 0, 0, tiled=True)
    w1, pair3 = lax.optimization_barrier((load(w1), pair3))
    pair4 = ring(pair3)
    grad_in = latents_grad(gp, gp_next, cross, inner, w1)
    far1, far2 = inside(pair1), inside(pair2)
    pair3, far1, far2, _ = lax.optimization_barrier((pair3, far1, far2, grad_in))
    blocks = (pair0, pair1, pair2, pair3, pair4, far1, far2, inside(pair3))

    one = one_part(g, g_next, blocks)
    one = lax.all_to_all(one, ("dp", "frame"), 0, 0, tiled=True)
    two = lax.all_to_all(two_mid(two), "height", 0, 0, tiled=True)
    one = final_one(one).reshape(3, 3, 3, 24, 24)
    two = jnp.swapaxes(final_two(two).reshape(3, 3, 12, 24), 2, 3)
    return (grad_in[None], one, two)


def solution(mesh):
    placed = (
        P("dp", "frame", "height", None, None),
        P(),
        P(),
        P("dp", "frame", "height", None, None),
    )
    return jax.shard_map(
        local,
        mesh=mesh,
        in_specs=placed,
        out_specs=(
            P("dp", "frame", "height", None, None),
            P(None, None, None, ("dp", "frame"), "height"),
            P(None, None, ("dp", "frame"), "height"),
        ),
        check_vma=False,
    )
```

```python
import jax
import jax.numpy as jnp
from jax import lax
from jax.experimental import pallas as pl
from jax.experimental.pallas import tpu as pltpu
from jax.sharding import PartitionSpec as P

BF = jnp.bfloat16
F32 = jnp.float32
MIB = 1024 * 1024


def params(mib=16):
    return pltpu.CompilerParams(vmem_limit_bytes=mib * MIB)


def anywhere(count):
    return [pl.BlockSpec(memory_space=pl.ANY)] * count


def bring(sources, targets, sems):
    copies = [
        pltpu.make_async_copy(source, target, sems.at[n])
        for n, (source, target) in enumerate(zip(sources, targets))
    ]
    for each in copies:
        each.start()
    return copies


def vmem(count):
    return [pl.BlockSpec(memory_space=pltpu.VMEM)] * count


def cost(macs, nbytes):
    return pl.CostEstimate(flops=2 * macs, bytes_accessed=nbytes, transcendentals=0)


def column_shifts(wide):
    row = lax.broadcasted_iota(jnp.int32, wide.shape, 0)
    before = jnp.where(row == 0, 0.0, pltpu.roll(wide, 1, 0))
    after = jnp.where(row == 63, 0.0, pltpu.roll(wide, 63, 0))
    return before.astype(BF), after.astype(BF)


def place():
    height, frame = lax.axis_index("height"), lax.axis_index("frame")
    last = lax.axis_size("height") - 1, lax.axis_size("frame") - 1
    return (
        lax.rem(height, 2),
        (height > 0).astype(F32),
        (height < last[0]).astype(F32),
        (frame > 0).astype(F32),
        (frame < last[1]).astype(F32),
    )


def stack_columns(dest, low, high, cross, inner, at, oks, order):
    core, above_ok, below_ok = at[:3]
    for f in range(4):
        for r in range(4):
            keep = oks[f // 2]
            if r in (0, 3):
                pick_cross = core == (0 if r == 0 else 1)
                block = jnp.where(pick_cross, cross[f].astype(F32), inner[f].astype(F32))
                edge = above_ok if r == 0 else below_ok
                keep = edge if keep is None else edge * keep
            else:
                block = (low if f < 2 else high)[f % 2, r - 1].astype(F32)
            if keep is not None:
                block = block * keep
            before, after = column_shifts(block)
            sides = (before, after) if order > 0 else (after, before)
            dest[f, r, :, 0:384] = sides[0]
            dest[f, r, :, 384:768] = block.astype(BF)
            dest[f, r, :, 768:1152] = sides[1]


def load_kernel(w, out, sems):
    parts = [pl.ds(3 * n, 3) for n in range(9)]
    for each in bring([w.at[p] for p in parts], [out.at[p] for p in parts], sems):
        each.wait()


def load(w):
    return pl.pallas_call(
        load_kernel,
        in_specs=anywhere(1),
        out_specs=vmem(1)[0],
        out_shape=jax.ShapeDtypeStruct((27, 384, 384), BF),
        scratch_shapes=[pltpu.SemaphoreType.DMA((9,))],
        compiler_params=params(46),
        cost_estimate=cost(1000, 16_000_000),
        name="load",
    )(w)


def pair_kernel(own, other, cot, out, cross, inner):
    core = place()[0]
    out[core] = own[...]
    out[1 - core] = other[...]
    for target, line in ((cross, 3 * core), (inner, 3 - 3 * core)):
        for t in range(2):
            for n in range(3):
                target[t, :, n * 128 : (n + 1) * 128] = cot[t, line, n * 64 : (n + 1) * 64, :]


def pair(own, other, cot):
    rows = jax.ShapeDtypeStruct((2, 64, 384), BF)
    return pl.pallas_call(
        pair_kernel,
        in_specs=vmem(3),
        out_specs=tuple(vmem(3)),
        out_shape=(jax.ShapeDtypeStruct((2, 2, 2, 64, 384), BF), rows, rows),
        compiler_params=params(),
        cost_estimate=cost(1000, 1_600_000),
        name="pair",
    )(own, other, cot)


def edges_kernel(own, prev, cot_cross, cot_inner, cross, inner):
    core = place()[0]
    for out, row, lines in ((cross, core, cot_cross), (inner, 1 - core, cot_inner)):
        for t in range(2):
            out[t] = prev[t, row]
            out[2 + t] = own[t, row]
            out[4 + t] = lines[t]


def edges(own, prev, cot_cross, cot_inner):
    shape = jax.ShapeDtypeStruct((6, 64, 384), BF)
    return pl.pallas_call(
        edges_kernel,
        in_specs=vmem(4),
        out_specs=tuple(vmem(2)),
        out_shape=(shape, shape),
        compiler_params=params(),
        cost_estimate=cost(1000, 1_000_000),
        name="edges",
    )(own, prev, cot_cross, cot_inner)


def box_pick():
    size = (64, 256)
    pos = lax.broadcasted_iota(jnp.int32, size, 1) & 127
    low = lax.broadcasted_iota(jnp.int32, size, 0)
    pick = []
    for k in range(3):
        offset = pos - 2 * low - 1 + k
        pick.append(jnp.where((offset == 0) | (offset == 1), 1.0, 0.0))
    return jnp.concatenate(pick, axis=0).astype(BF)


def forward_kernel(
    own, prev, cross, inner, cotv, w2, wv, gp, gpt, ht, keep, give, xx, gcat, w2v, sems
):
    last = bring([w2.at[:, pl.ds(0, 96)], w2.at[:, pl.ds(96, 96)]], [w2v.at[0], w2v.at[1]], sems)
    at = place()
    core, above_ok, below_ok, before_ok = at[:4]
    stack_columns(xx, prev, own, cross, inner, at, (before_ok, None), 1)

    def line(t, r):
        if 0 <= r < 4:
            return cotv[t, r]
        pick_cross = core == (0 if r < 0 else 1)
        row = jnp.where(pick_cross, cross[4 + t].astype(F32), inner[4 + t].astype(F32))
        row = (row * (above_ok if r < 0 else below_ok)).astype(BF)
        return jnp.concatenate([row[:, n * 128 : (n + 1) * 128] for n in range(3)], axis=0)

    pick = box_pick()
    for t in range(2):
        for r in range(2):
            rows = pl.ds((t * 2 + r) * 64, 64)
            for j in range(3):
                a = 2 * r + 1 - j
                pair = jnp.concatenate([line(t, a), line(t, a + 1)], axis=1)
                box = lax.dot_general(
                    pick, pair, (((1,), (1,)), ((), ())), preferred_element_type=F32
                ).astype(BF)
                for k in range(3):
                    for half in range(2):
                        piece = box[k * 64 : (k + 1) * 64, half * 96 : half * 96 + 96]
                        gcat[half, rows, pl.ds((j * 3 + k) * 96, 96)] = piece
    pre = jnp.zeros((256, 384), F32)
    for n in range(9):
        i, j = n // 3, n % 3
        lhs = xx[i : i + 2, j : j + 2].reshape(256, 1152)
        rhs = wv[3 * n : 3 * n + 3].reshape(1152, 384)
        pre = pre + jnp.dot(lhs, rhs, preferred_element_type=F32)
    keep[...] = gcat[core]
    give[...] = gcat[1 - core]
    for each in last:
        each.wait()
    gh = jnp.zeros((256, 384), F32)
    for half in range(2):
        rhs = w2v[half].reshape(864, 384)
        gh = gh + jnp.dot(gcat[half], rhs, preferred_element_type=F32)
    sigma = jax.nn.sigmoid(pre)
    hidden = pre * sigma
    grad = gh * sigma * (1.0 + pre * (1.0 - sigma))
    gp[...] = grad.astype(BF).reshape(2, 2, 64, 384)
    grad_t = grad.T
    for b in range(16):
        gpt[b] = grad_t[b * 24 : (b + 1) * 24].astype(BF)
    ht[...] = hidden.T.astype(BF)


def forward(own, prev, cross, inner, cot, w2, w):
    return pl.pallas_call(
        forward_kernel,
        in_specs=vmem(5) + anywhere(1) + vmem(1),
        out_specs=tuple(vmem(5)),
        out_shape=(
            jax.ShapeDtypeStruct((2, 2, 64, 384), BF),
            jax.ShapeDtypeStruct((16, 24, 256), BF),
            jax.ShapeDtypeStruct((384, 256), BF),
            jax.ShapeDtypeStruct((256, 864), BF),
            jax.ShapeDtypeStruct((256, 864), BF),
        ),
        scratch_shapes=[
            pltpu.VMEM((4, 4, 64, 1152), BF),
            pltpu.VMEM((2, 256, 864), BF),
            pltpu.VMEM((2, 9, 96, 384), BF),
            pltpu.SemaphoreType.DMA((2,)),
        ],
        compiler_params=params(14),
        cost_estimate=cost(1_300_000_000, 12_000_000),
        name="forward",
    )(own, prev, cross, inner, cot, w2, w)


def rows_kernel(own, after, cross, inner):
    core = place()[0]
    for out, row in ((cross, core), (inner, 1 - core)):
        for t in range(2):
            out[t] = own[t, row]
            out[2 + t] = after[t, row]


def rows(own, after):
    shape = jax.ShapeDtypeStruct((4, 64, 384), BF)
    return pl.pallas_call(
        rows_kernel,
        in_specs=vmem(2),
        out_specs=tuple(vmem(2)),
        out_shape=(shape, shape),
        compiler_params=params(),
        cost_estimate=cost(1000, 800_000),
        name="rows",
    )(own, after)


def two_kernel(ht, keep, ht_other, given, out):
    res = jnp.dot(ht[...], keep[...], preferred_element_type=F32)
    res = res + jnp.dot(ht_other[...], given[...], preferred_element_type=F32)
    for b in range(16):
        out[b] = res[b * 24 : (b + 1) * 24].astype(BF)


def two_part(ht, keep, ht_other, given):
    return pl.pallas_call(
        two_kernel,
        in_specs=vmem(4),
        out_specs=vmem(1)[0],
        out_shape=jax.ShapeDtypeStruct((16, 24, 864), BF),
        compiler_params=params(),
        cost_estimate=cost(170_000_000, 3_000_000),
        name="two_part",
    )(ht, keep, ht_other, given)


def latents_kernel(own, after, cross, inner, wv, out, gg):
    at = place()
    stack_columns(gg, own, after, cross, inner, at, (None, at[4]), -1)
    total = jnp.zeros((256, 384), F32)
    for n in range(9):
        i, j = n // 3, n % 3
        lhs = gg[2 - i : 4 - i, 2 - j : 4 - j].reshape(256, 1152)
        rhs = jnp.concatenate([wv[3 * n], wv[3 * n + 1], wv[3 * n + 2]], axis=1)
        total = total + lax.dot_general(
            lhs, rhs, (((1,), (1,)), ((), ())), preferred_element_type=F32
        )
    out[...] = total.astype(BF).reshape(2, 2, 64, 384)


def latents_grad(own, after, cross, inner, w):
    return pl.pallas_call(
        latents_kernel,
        in_specs=vmem(5),
        out_specs=vmem(1)[0],
        out_shape=jax.ShapeDtypeStruct((2, 2, 64, 384), BF),
        scratch_shapes=[
            pltpu.VMEM((4, 4, 64, 1152), BF),
        ],
        compiler_params=params(12),
        cost_estimate=cost(1_020_000_000, 10_000_000),
        name="latents_grad",
    )(own, after, cross, inner, w)


def one_kernel(g_in, g_after_in, *rest):
    blocks, (out, gs, cols, xv, g, g_after, sems) = rest[:8], rest[8:]
    arrive = bring(
        (g_in, g_after_in) + blocks, [g, g_after] + [xv.at[n] for n in range(8)], sems
    )
    arrive[0].wait()
    arrive[1].wait()
    lane = lax.broadcasted_iota(jnp.int32, (24, 128), 1)
    col = lane & 63
    left = lane < 64
    height = lax.axis_index("height")
    chip = height // 2
    way = 1 - 2 * (height - 2 * chip)

    after_ok = place()[4]
    cols[0] = jnp.zeros((4, 3, 24, 128), F32)
    cols[17] = jnp.zeros((4, 3, 24, 128), F32)
    for h in range(16):
        for f in range(4):
            mid = (g if f < 2 else g_after)[h, :, pl.ds(f % 2 * 128, 128)].astype(F32)
            mid = mid if f < 2 else mid * after_ok
            cols[h + 1, f, 0] = jnp.where(col == 63, 0.0, pltpu.roll(mid, 127, 1))
            cols[h + 1, f, 1] = mid
            cols[h + 1, f, 2] = jnp.where(col == 0, 0.0, pltpu.roll(mid, 1, 1))
    for n, steps in enumerate((0, -1, -2, -3, 4, 1, 2, 3)):
        at = 2 * lax.rem(chip + way * steps + 16, 8)
        for f in range(4):
            lines = [[cols[at + m, f, k] for k in range(3)] for m in range(4)]
            for m in range(2):
                above, here, below = lines[m : m + 3]
                rows = [pltpu.roll(jnp.where(left, b, a), 64, 1) for a, b in zip(here, below)]
                rows += here
                rows += [pltpu.roll(jnp.where(left, b, a), 64, 1) for a, b in zip(above, here)]
                rows.append(jnp.zeros((8, 128), F32))
                to = pl.ds((2 * n + m) * 128, 128)
                gs[f, :, to] = jnp.concatenate(rows, axis=0).astype(BF)

    for each in arrive[2:]:
        each.wait()
    total = jnp.zeros((672, 384), F32)
    for s in range(2):
        xs = xv[:, :, s].reshape(2048, 384)
        lhs = gs[s : s + 3].reshape(672, 2048)
        total = total + jnp.dot(lhs, xs, preferred_element_type=F32)
    pad = jnp.zeros((32, 384), F32)
    for b in range(3):
        turned = jnp.concatenate([total[b * 224 : (b + 1) * 224], pad], axis=0).T
        for c in range(16):
            out[c, :, b * 256 : (b + 1) * 256] = turned[c * 24 : (c + 1) * 24].astype(BF)


def one_part(g, g_after, blocks):
    return pl.pallas_call(
        one_kernel,
        in_specs=anywhere(10),
        out_specs=vmem(1)[0],
        out_shape=jax.ShapeDtypeStruct((16, 24, 768), BF),
        scratch_shapes=[
            pltpu.VMEM((4, 224, 2048), BF),
            pltpu.VMEM((18, 4, 3, 24, 128), F32),
            pltpu.VMEM((8, 2, 2, 2, 64, 384), BF),
            pltpu.VMEM((16, 24, 256), BF),
            pltpu.VMEM((16, 24, 256), BF),
            pltpu.SemaphoreType.DMA((10,)),
        ],
        compiler_params=params(20),
        cost_estimate=cost(1_020_000_000, 5_000_000),
        name="one_part",
    )(g, g_after, *blocks)


def summed(ref):
    total = ref[0].astype(F32)
    for n in range(1, 16):
        total = total + ref[n].astype(F32)
    return total


def two_mid_kernel(parts, out):
    core = place()[0]
    total = summed(parts)
    pad = jnp.zeros((24, 20), F32)
    for h in range(8):
        cut = [total[:, n * 96 + h * 12 : n * 96 + h * 12 + 12] for n in range(9)]
        out[core * 8 + h] = jnp.concatenate(cut + [pad], axis=1).astype(BF)
        out[8 - core * 8 + h] = jnp.zeros((24, 128), BF)


def two_mid(parts):
    return pl.pallas_call(
        two_mid_kernel,
        out_shape=jax.ShapeDtypeStruct((16, 24, 128), BF),
        compiler_params=params(),
        cost_estimate=cost(1_000_000, 1_500_000),
        name="two_mid",
    )(parts)


def final_one_kernel(parts, out):
    total = summed(parts)
    for i in range(3):
        for n in range(9):
            at = (2 - i) * 256 + n * 24
            out[i * 9 + n] = total[:, at : at + 24]


def final_one(parts):
    return pl.pallas_call(
        final_one_kernel,
        out_shape=jax.ShapeDtypeStruct((27, 24, 24), F32),
        compiler_params=params(),
        cost_estimate=cost(1_000_000, 800_000),
        name="final_one",
    )(parts)


def final_two_kernel(parts, out):
    turned = summed(parts).T
    for n in range(9):
        out[n] = turned[n * 12 : (n + 1) * 12]


def final_two(parts):
    return pl.pallas_call(
        final_two_kernel,
        out_shape=jax.ShapeDtypeStruct((9, 12, 24), F32),
        compiler_params=params(),
        cost_estimate=cost(1_000_000, 200_000),
        name="final_two",
    )(parts)


def local(clip_latents, conv_one, conv_two, cotangent):
    x = clip_latents[0]
    cot = cotangent[0]
    heights = lax.axis_size("height")
    frames = lax.axis_size("frame")
    next_perm = [(n, (n + 1) % frames) for n in range(frames)]
    prev_perm = [((n + 1) % frames, n) for n in range(frames)]
    inner_perm = [(n, n ^ 1) for n in range(heights)]
    cross_perm = [(n, (n + 1 if n % 2 else n - 1) % heights) for n in range(heights)]
    ring_perm = [(n, (n - 2 if n % 2 else n + 2) % heights) for n in range(heights)]

    def inside(value):
        return lax.ppermute(value, "height", inner_perm)

    def across(value):
        return lax.ppermute(value, "height", cross_perm)

    def ring(value):
        return lax.ppermute(value, "height", ring_perm)

    cot = jnp.swapaxes(cot, 2, 3)
    w1 = conv_one.reshape(27, 384, 384)
    w2 = jnp.swapaxes(conv_two, 2, 3).reshape(9, 192, 384)
    x_prev = lax.ppermute(x, "frame", next_perm)
    pair0, cot_cross, cot_inner = pair(x, inside(x), cot)
    pair1 = ring(pair0)
    cross, inner = edges(x, x_prev, cot_cross, cot_inner)
    w1_first, cross, inner = lax.optimization_barrier((w1, cross, inner))
    w1_first = load(w1_first)
    cross, inner = across(cross), inside(inner)
    pair1, w1_first, cross, inner = lax.optimization_barrier((pair1, w1_first, cross, inner))
    pair2 = ring(pair1)
    gp, gpt, ht, keep, give = forward(x, x_prev, cross, inner, cot, w2, w1_first)

    gp_next = lax.ppermute(gp, "frame", prev_perm)
    g = lax.all_to_all(gpt, "height", 0, 0, tiled=True)
    ht_other, given = inside(ht), inside(give)
    gp_next, pair2 = lax.optimization_barrier((gp_next, pair2))
    g_next = lax.ppermute(g, "frame", prev_perm)
    ht, pair2, gp_next, _ = lax.optimization_barrier((ht, pair2, gp_next, g))
    two = two_part(ht, keep, ht_other, given)
    pair2, _ = lax.optimization_barrier((pair2, two))
    pair3 = ring(pair2)
    two = lax.all_to_all(two, ("dp", "frame"), 0, 0, tiled=True)
    far1, far2 = inside(pair1), inside(pair2)
    pair3, gp_next, far1, far2 = lax.optimization_barrier((pair3, gp_next, far1, far2))
    pair4, far3 = ring(pair3), inside(pair3)
    cross, inner = rows(gp, gp_next)
    cross, inner = across(cross), inside(inner)
    two, far3 = lax.optimization_barrier((two, far3))
    two = lax.all_to_all(two_mid(two), "height", 0, 0, tiled=True)
    blocks = (pair0, pair1, pair2, pair3, pair4, far1, far2, far3)

    one = one_part(g, g_next, blocks)
    one, w1, cross, inner = lax.optimization_barrier((one, w1, cross, inner))
    one = lax.all_to_all(one, ("dp", "frame"), 0, 0, tiled=True)
    grad_in = latents_grad(gp, gp_next, cross, inner, load(w1))
    one = final_one(one).reshape(3, 3, 3, 24, 24)
    two = jnp.swapaxes(final_two(two).reshape(3, 3, 12, 24), 2, 3)
    return (grad_in[None], one, two)


def solution(mesh):
    placed = (
        P("dp", "frame", "height", None, None),
        P(),
        P(),
        P("dp", "frame", "height", None, None),
    )
    return jax.shard_map(
        local,
        mesh=mesh,
        in_specs=placed,
        out_specs=(
            P("dp", "frame", "height", None, None),
            P(None, None, None, ("dp", "frame"), "height"),
            P(None, None, ("dp", "frame"), "height"),
        ),
        check_vma=False,
    )
```

```python
import jax
import jax.numpy as jnp
from jax import lax
from jax.experimental import pallas as pl
from jax.experimental.pallas import tpu as pltpu
from jax.sharding import PartitionSpec as P

BF = jnp.bfloat16
F32 = jnp.float32
MIB = 1024 * 1024


def params(mib=16):
    return pltpu.CompilerParams(vmem_limit_bytes=mib * MIB)


def anywhere(count):
    return [pl.BlockSpec(memory_space=pl.ANY)] * count


def bring(sources, targets, sems):
    copies = [
        pltpu.make_async_copy(source, target, sems.at[n])
        for n, (source, target) in enumerate(zip(sources, targets))
    ]
    for each in copies:
        each.start()
    return copies


def vmem(count):
    return [pl.BlockSpec(memory_space=pltpu.VMEM)] * count


def cost(macs, nbytes):
    return pl.CostEstimate(flops=2 * macs, bytes_accessed=nbytes, transcendentals=0)


def column_shifts(wide):
    row = lax.broadcasted_iota(jnp.int32, wide.shape, 0)
    before = jnp.where(row == 0, 0.0, pltpu.roll(wide, 1, 0))
    after = jnp.where(row == 63, 0.0, pltpu.roll(wide, 63, 0))
    return before.astype(BF), after.astype(BF)


def place():
    height, frame = lax.axis_index("height"), lax.axis_index("frame")
    last = lax.axis_size("height") - 1, lax.axis_size("frame") - 1
    return (
        lax.rem(height, 2),
        (height > 0).astype(F32),
        (height < last[0]).astype(F32),
        (frame > 0).astype(F32),
        (frame < last[1]).astype(F32),
    )


def stack_columns(dest, low, high, cross, inner, at, oks, order):
    core, above_ok, below_ok = at[:3]
    for f in range(4):
        for r in range(4):
            keep = oks[f // 2]
            if r in (0, 3):
                pick_cross = core == (0 if r == 0 else 1)
                block = jnp.where(pick_cross, cross[f].astype(F32), inner[f].astype(F32))
                edge = above_ok if r == 0 else below_ok
                keep = edge if keep is None else edge * keep
            else:
                block = (low if f < 2 else high)[f % 2, r - 1].astype(F32)
            if keep is not None:
                block = block * keep
            before, after = column_shifts(block)
            sides = (before, after) if order > 0 else (after, before)
            dest[f, r, :, 0:384] = sides[0]
            dest[f, r, :, 384:768] = block.astype(BF)
            dest[f, r, :, 768:1152] = sides[1]


def load_kernel(w, out, sems):
    parts = [pl.ds(3 * n, 3) for n in range(9)]
    for each in bring([w.at[p] for p in parts], [out.at[p] for p in parts], sems):
        each.wait()


def load(w):
    return pl.pallas_call(
        load_kernel,
        in_specs=anywhere(1),
        out_specs=vmem(1)[0],
        out_shape=jax.ShapeDtypeStruct((27, 384, 384), BF),
        scratch_shapes=[pltpu.SemaphoreType.DMA((9,))],
        compiler_params=params(46),
        cost_estimate=cost(1000, 16_000_000),
        name="load",
    )(w)


def pair_kernel(own, other, cot, out, cross, inner):
    core = place()[0]
    out[core] = own[...]
    out[1 - core] = other[...]
    for target, line in ((cross, 3 * core), (inner, 3 - 3 * core)):
        for t in range(2):
            for n in range(3):
                target[t, :, n * 128 : (n + 1) * 128] = cot[t, line, n * 64 : (n + 1) * 64, :]


def pair(own, other, cot):
    rows = jax.ShapeDtypeStruct((2, 64, 384), BF)
    return pl.pallas_call(
        pair_kernel,
        in_specs=vmem(3),
        out_specs=tuple(vmem(3)),
        out_shape=(jax.ShapeDtypeStruct((2, 2, 2, 64, 384), BF), rows, rows),
        compiler_params=params(),
        cost_estimate=cost(1000, 1_600_000),
        name="pair",
    )(own, other, cot)


def edges_kernel(own, prev, cot_cross, cot_inner, cross, inner):
    core = place()[0]
    for out, row, lines in ((cross, core, cot_cross), (inner, 1 - core, cot_inner)):
        for t in range(2):
            out[t] = prev[t, row]
            out[2 + t] = own[t, row]
            out[4 + t] = lines[t]


def edges(own, prev, cot_cross, cot_inner):
    shape = jax.ShapeDtypeStruct((6, 64, 384), BF)
    return pl.pallas_call(
        edges_kernel,
        in_specs=vmem(4),
        out_specs=tuple(vmem(2)),
        out_shape=(shape, shape),
        compiler_params=params(),
        cost_estimate=cost(1000, 1_000_000),
        name="edges",
    )(own, prev, cot_cross, cot_inner)


def box_pick():
    size = (64, 256)
    pos = lax.broadcasted_iota(jnp.int32, size, 1) & 127
    low = lax.broadcasted_iota(jnp.int32, size, 0)
    pick = []
    for k in range(3):
        offset = pos - 2 * low - 1 + k
        pick.append(jnp.where((offset == 0) | (offset == 1), 1.0, 0.0))
    return jnp.concatenate(pick, axis=0).astype(BF)


def forward_kernel(
    own, prev, cross, inner, cotv, w2, wv, gp, gpt, ht, keep, give, xx, gcat, w2v, sems
):
    last = bring([w2.at[:, pl.ds(0, 96)], w2.at[:, pl.ds(96, 96)]], [w2v.at[0], w2v.at[1]], sems)
    at = place()
    core, above_ok, below_ok, before_ok = at[:4]
    stack_columns(xx, prev, own, cross, inner, at, (before_ok, None), 1)

    def line(t, r):
        if 0 <= r < 4:
            return cotv[t, r]
        pick_cross = core == (0 if r < 0 else 1)
        row = jnp.where(pick_cross, cross[4 + t].astype(F32), inner[4 + t].astype(F32))
        row = (row * (above_ok if r < 0 else below_ok)).astype(BF)
        return jnp.concatenate([row[:, n * 128 : (n + 1) * 128] for n in range(3)], axis=0)

    pick = box_pick()
    for t in range(2):
        for r in range(2):
            rows = pl.ds((t * 2 + r) * 64, 64)
            for j in range(3):
                a = 2 * r + 1 - j
                pair = jnp.concatenate([line(t, a), line(t, a + 1)], axis=1)
                box = lax.dot_general(
                    pick, pair, (((1,), (1,)), ((), ())), preferred_element_type=F32
                ).astype(BF)
                for k in range(3):
                    for half in range(2):
                        piece = box[k * 64 : (k + 1) * 64, half * 96 : half * 96 + 96]
                        gcat[half, rows, pl.ds((j * 3 + k) * 96, 96)] = piece
    pre = jnp.zeros((256, 384), F32)
    for n in range(9):
        i, j = n // 3, n % 3
        lhs = xx[i : i + 2, j : j + 2].reshape(256, 1152)
        rhs = wv[3 * n : 3 * n + 3].reshape(1152, 384)
        pre = pre + jnp.dot(lhs, rhs, preferred_element_type=F32)
    keep[...] = gcat[core]
    give[...] = gcat[1 - core]
    for each in last:
        each.wait()
    gh = jnp.zeros((256, 384), F32)
    for half in range(2):
        rhs = w2v[half].reshape(864, 384)
        gh = gh + jnp.dot(gcat[half], rhs, preferred_element_type=F32)
    sigma = jax.nn.sigmoid(pre)
    hidden = pre * sigma
    grad = gh * sigma * (1.0 + pre * (1.0 - sigma))
    gp[...] = grad.astype(BF).reshape(2, 2, 64, 384)
    grad_t = grad.T
    for b in range(16):
        gpt[b] = grad_t[b * 24 : (b + 1) * 24].astype(BF)
    ht[...] = hidden.T.astype(BF)


def forward(own, prev, cross, inner, cot, w2, w):
    return pl.pallas_call(
        forward_kernel,
        in_specs=vmem(5) + anywhere(1) + vmem(1),
        out_specs=tuple(vmem(5)),
        out_shape=(
            jax.ShapeDtypeStruct((2, 2, 64, 384), BF),
            jax.ShapeDtypeStruct((16, 24, 256), BF),
            jax.ShapeDtypeStruct((384, 256), BF),
            jax.ShapeDtypeStruct((256, 864), BF),
            jax.ShapeDtypeStruct((256, 864), BF),
        ),
        scratch_shapes=[
            pltpu.VMEM((4, 4, 64, 1152), BF),
            pltpu.VMEM((2, 256, 864), BF),
            pltpu.VMEM((2, 9, 96, 384), BF),
            pltpu.SemaphoreType.DMA((2,)),
        ],
        compiler_params=params(14),
        cost_estimate=cost(1_300_000_000, 12_000_000),
        name="forward",
    )(own, prev, cross, inner, cot, w2, w)


def rows_kernel(own, after, cross, inner):
    core = place()[0]
    for out, row in ((cross, core), (inner, 1 - core)):
        for t in range(2):
            out[t] = own[t, row]
            out[2 + t] = after[t, row]


def rows(own, after):
    shape = jax.ShapeDtypeStruct((4, 64, 384), BF)
    return pl.pallas_call(
        rows_kernel,
        in_specs=vmem(2),
        out_specs=tuple(vmem(2)),
        out_shape=(shape, shape),
        compiler_params=params(),
        cost_estimate=cost(1000, 800_000),
        name="rows",
    )(own, after)


def two_kernel(ht, keep, ht_other, given, out):
    res = jnp.dot(ht[...], keep[...], preferred_element_type=F32)
    res = res + jnp.dot(ht_other[...], given[...], preferred_element_type=F32)
    for b in range(16):
        out[b] = res[b * 24 : (b + 1) * 24].astype(BF)


def two_part(ht, keep, ht_other, given):
    return pl.pallas_call(
        two_kernel,
        in_specs=vmem(4),
        out_specs=vmem(1)[0],
        out_shape=jax.ShapeDtypeStruct((16, 24, 864), BF),
        compiler_params=params(),
        cost_estimate=cost(170_000_000, 3_000_000),
        name="two_part",
    )(ht, keep, ht_other, given)


def latents_kernel(own, after, cross, inner, wv, out, gg):
    at = place()
    stack_columns(gg, own, after, cross, inner, at, (None, at[4]), -1)
    total = jnp.zeros((256, 384), F32)
    for n in range(9):
        i, j = n // 3, n % 3
        lhs = gg[2 - i : 4 - i, 2 - j : 4 - j].reshape(256, 1152)
        rhs = jnp.concatenate([wv[3 * n], wv[3 * n + 1], wv[3 * n + 2]], axis=1)
        total = total + lax.dot_general(
            lhs, rhs, (((1,), (1,)), ((), ())), preferred_element_type=F32
        )
    out[...] = total.astype(BF).reshape(2, 2, 64, 384)


def latents_grad(own, after, cross, inner, w):
    return pl.pallas_call(
        latents_kernel,
        in_specs=vmem(5),
        out_specs=vmem(1)[0],
        out_shape=jax.ShapeDtypeStruct((2, 2, 64, 384), BF),
        scratch_shapes=[
            pltpu.VMEM((4, 4, 64, 1152), BF),
        ],
        compiler_params=params(12),
        cost_estimate=cost(1_020_000_000, 10_000_000),
        name="latents_grad",
    )(own, after, cross, inner, w)


def one_kernel(g_in, g_after_in, *rest):
    blocks, (out, gs, cols, xv, g, g_after, sems) = rest[:8], rest[8:]
    arrive = bring(
        (g_in, g_after_in) + blocks, [g, g_after] + [xv.at[n] for n in range(8)], sems
    )
    arrive[0].wait()
    arrive[1].wait()
    lane = lax.broadcasted_iota(jnp.int32, (24, 128), 1)
    col = lane & 63
    left = lane < 64
    height = lax.axis_index("height")
    chip = height // 2
    way = 1 - 2 * (height - 2 * chip)

    after_ok = place()[4]
    cols[0] = jnp.zeros((4, 3, 24, 128), F32)
    cols[17] = jnp.zeros((4, 3, 24, 128), F32)
    for h in range(16):
        for f in range(4):
            mid = (g if f < 2 else g_after)[h, :, pl.ds(f % 2 * 128, 128)].astype(F32)
            mid = mid if f < 2 else mid * after_ok
            cols[h + 1, f, 0] = jnp.where(col == 63, 0.0, pltpu.roll(mid, 127, 1))
            cols[h + 1, f, 1] = mid
            cols[h + 1, f, 2] = jnp.where(col == 0, 0.0, pltpu.roll(mid, 1, 1))
    for n, steps in enumerate((0, -1, -2, -3, 4, 1, 2, 3)):
        at = 2 * lax.rem(chip + way * steps + 16, 8)
        for f in range(4):
            lines = [[cols[at + m, f, k] for k in range(3)] for m in range(4)]
            for m in range(2):
                above, here, below = lines[m : m + 3]
                rows = [pltpu.roll(jnp.where(left, b, a), 64, 1) for a, b in zip(here, below)]
                rows += here
                rows += [pltpu.roll(jnp.where(left, b, a), 64, 1) for a, b in zip(above, here)]
                rows.append(jnp.zeros((8, 128), F32))
                to = pl.ds((2 * n + m) * 128, 128)
                gs[f, :, to] = jnp.concatenate(rows, axis=0).astype(BF)

    for each in arrive[2:]:
        each.wait()
    total = jnp.zeros((672, 384), F32)
    for s in range(2):
        xs = xv[:, :, s].reshape(2048, 384)
        lhs = gs[s : s + 3].reshape(672, 2048)
        total = total + jnp.dot(lhs, xs, preferred_element_type=F32)
    pad = jnp.zeros((32, 384), F32)
    for b in range(3):
        turned = jnp.concatenate([total[b * 224 : (b + 1) * 224], pad], axis=0).T
        for c in range(16):
            out[c, :, b * 256 : (b + 1) * 256] = turned[c * 24 : (c + 1) * 24].astype(BF)


def one_part(g, g_after, blocks):
    return pl.pallas_call(
        one_kernel,
        in_specs=anywhere(10),
        out_specs=vmem(1)[0],
        out_shape=jax.ShapeDtypeStruct((16, 24, 768), BF),
        scratch_shapes=[
            pltpu.VMEM((4, 224, 2048), BF),
            pltpu.VMEM((18, 4, 3, 24, 128), F32),
            pltpu.VMEM((8, 2, 2, 2, 64, 384), BF),
            pltpu.VMEM((16, 24, 256), BF),
            pltpu.VMEM((16, 24, 256), BF),
            pltpu.SemaphoreType.DMA((10,)),
        ],
        compiler_params=params(20),
        cost_estimate=cost(1_020_000_000, 5_000_000),
        name="one_part",
    )(g, g_after, *blocks)


def summed(ref):
    total = ref[0].astype(F32)
    for n in range(1, 16):
        total = total + ref[n].astype(F32)
    return total


def two_mid_kernel(parts, out):
    core = place()[0]
    total = summed(parts)
    pad = jnp.zeros((24, 20), F32)
    for h in range(8):
        cut = [total[:, n * 96 + h * 12 : n * 96 + h * 12 + 12] for n in range(9)]
        out[core * 8 + h] = jnp.concatenate(cut + [pad], axis=1).astype(BF)
        out[8 - core * 8 + h] = jnp.zeros((24, 128), BF)


def two_mid(parts):
    return pl.pallas_call(
        two_mid_kernel,
        out_shape=jax.ShapeDtypeStruct((16, 24, 128), BF),
        compiler_params=params(),
        cost_estimate=cost(1_000_000, 1_500_000),
        name="two_mid",
    )(parts)


def final_one_kernel(parts, out):
    total = summed(parts)
    for i in range(3):
        for n in range(9):
            at = (2 - i) * 256 + n * 24
            out[i * 9 + n] = total[:, at : at + 24]


def final_one(parts):
    return pl.pallas_call(
        final_one_kernel,
        out_shape=jax.ShapeDtypeStruct((27, 24, 24), F32),
        compiler_params=params(),
        cost_estimate=cost(1_000_000, 800_000),
        name="final_one",
    )(parts)


def final_two_kernel(parts, out):
    turned = summed(parts).T
    for n in range(9):
        out[n] = turned[n * 12 : (n + 1) * 12]


def final_two(parts):
    return pl.pallas_call(
        final_two_kernel,
        out_shape=jax.ShapeDtypeStruct((9, 12, 24), F32),
        compiler_params=params(),
        cost_estimate=cost(1_000_000, 200_000),
        name="final_two",
    )(parts)


def local(clip_latents, conv_one, conv_two, cotangent):
    x = clip_latents[0]
    cot = cotangent[0]
    heights = lax.axis_size("height")
    frames = lax.axis_size("frame")
    next_perm = [(n, (n + 1) % frames) for n in range(frames)]
    prev_perm = [((n + 1) % frames, n) for n in range(frames)]
    inner_perm = [(n, n ^ 1) for n in range(heights)]
    cross_perm = [(n, (n + 1 if n % 2 else n - 1) % heights) for n in range(heights)]
    ring_perm = [(n, (n - 2 if n % 2 else n + 2) % heights) for n in range(heights)]

    def inside(value):
        return lax.ppermute(value, "height", inner_perm)

    def across(value):
        return lax.ppermute(value, "height", cross_perm)

    def ring(value):
        return lax.ppermute(value, "height", ring_perm)

    cot = jnp.swapaxes(cot, 2, 3)
    w1 = conv_one.reshape(27, 384, 384)
    w2 = jnp.swapaxes(conv_two, 2, 3).reshape(9, 192, 384)
    x_prev = lax.ppermute(x, "frame", next_perm)
    pair0, cot_cross, cot_inner = pair(x, inside(x), cot)
    pair1 = ring(pair0)
    cross, inner = edges(x, x_prev, cot_cross, cot_inner)
    w1_first, cross, inner = lax.optimization_barrier((w1, cross, inner))
    w1_first = load(w1_first)
    cross, inner = across(cross), inside(inner)
    pair1, w1_first, cross, inner = lax.optimization_barrier((pair1, w1_first, cross, inner))
    pair2 = ring(pair1)
    gp, gpt, ht, keep, give = forward(x, x_prev, cross, inner, cot, w2, w1_first)

    gp_next = lax.ppermute(gp, "frame", prev_perm)
    g = lax.all_to_all(gpt, "height", 0, 0, tiled=True)
    pair2, _ = lax.optimization_barrier((pair2, gp_next))
    pair3 = ring(pair2)
    ht_other, given = inside(ht), inside(give)
    cross, inner = rows(gp, gp_next)
    cross, inner = across(cross), inside(inner)
    g_next = lax.ppermute(g, "frame", prev_perm)
    ht, _, _ = lax.optimization_barrier((ht, gp_next, g))
    two = two_part(ht, keep, ht_other, given)
    pair3, _ = lax.optimization_barrier((pair3, two))
    two = lax.all_to_all(two, ("dp", "frame"), 0, 0, tiled=True)
    pair4 = ring(pair3)
    far1, far2 = inside(pair1), inside(pair2)
    two, far1, far2 = lax.optimization_barrier((two, far1, far2))
    blocks = (pair0, pair1, pair2, pair3, pair4, far1, far2, inside(pair3))

    two = lax.all_to_all(two_mid(two), "height", 0, 0, tiled=True)
    one = one_part(g, g_next, blocks)
    one, w1, cross, inner = lax.optimization_barrier((one, w1, cross, inner))
    one = lax.all_to_all(one, ("dp", "frame"), 0, 0, tiled=True)
    grad_in = latents_grad(gp, gp_next, cross, inner, load(w1))
    one = final_one(one).reshape(3, 3, 3, 24, 24)
    two = jnp.swapaxes(final_two(two).reshape(3, 3, 12, 24), 2, 3)
    return (grad_in[None], one, two)


def solution(mesh):
    placed = (
        P("dp", "frame", "height", None, None),
        P(),
        P(),
        P("dp", "frame", "height", None, None),
    )
    return jax.shard_map(
        local,
        mesh=mesh,
        in_specs=placed,
        out_specs=(
            P("dp", "frame", "height", None, None),
            P(None, None, None, ("dp", "frame"), "height"),
            P(None, None, ("dp", "frame"), "height"),
        ),
        check_vma=False,
    )
```
